128 devices in a mesh: gx: 4 (over x), yz: 32 (over z, y, core).
Axes of the slice: x: 4, y: 4, z: 4, core: 2. Of those that a mesh axis runs over, the one named last changes fastest.
Arguments:
- tokens: bfloat16 [4, 256, 18432], P('gx', None, 'yz'), may hold values from -6 to 6
- gain: float32 [18432], replicated, may hold values from 0.1 to 1.9
- w_query: bfloat16 [18432, 8192], P('gx', 'yz'), may hold values from -0.046875 to 0.046875
- w_keyval: bfloat16 [18432, 512], P('gx', 'yz'), may hold values from -0.09375 to 0.09375
- w_out: bfloat16 [8192, 18432], P('gx', 'yz'), may hold values from -0.375 to 0.375
- cache: bfloat16 [4, 2048, 512], P('gx', 'yz'), as said below
- lengths: int32 [4], P('gx'), may hold values from 1024 to 2048, as said below
Outputs:
- attended: bfloat16 [4, 256, 18432], P('gx', None, 'yz')
The draws below stay inside these ranges and needn't reach their ends.
Inputs may be any that keep to these rules, and one draw needn't show every extreme that they name: `lengths`: some sequence has exactly 2048 filled slots and some exactly 1024. `cache`: cached keys are already rotated to their slot positions.
All inputs are finite; a program needn't handle non-finite values.
Results may differ from the reference program's by a relative error of at most 0.012.
The reference program's roundings to bfloat16 on the way count: a program that leaves them out, or rounds other values in their place, can miss the bound.
Values may be sent and summed in bfloat16 or wider, within the bound.
A program may use at most 128 MiB of HBM per device.

```python
import math
import jax
import jax.numpy as jnp
from jax import lax

D = 18432
HEAD = 256
HEADS = 32
SPAN = 256
CACHE = 2048
BATCH = 4
QWIDTH = 8192


def draw_lengths(key, part):
    key = jax.random.fold_in(key, 7)
    first, second = jax.random.split(key)
    filled = jax.random.randint(first, (BATCH,), CACHE // 2, CACHE + 1)
    order = jax.random.permutation(second, BATCH)
    filled = filled.at[order[0]].set(CACHE)
    filled = filled.at[order[1]].set(CACHE // 2)
    return filled.astype(jnp.int32)


def draw_cache(key, part):
    key = jax.random.fold_in(key, 11)
    keys_list = jax.random.split(key, 4)
    stored_keys = 2.0 * jax.random.normal(keys_list[2], (BATCH, CACHE, HEAD), jnp.float32)
    stored_values = jax.random.normal(keys_list[3], (BATCH, CACHE, HEAD), jnp.float32)
    return jnp.concatenate([stored_keys, stored_values], axis=-1).astype(jnp.bfloat16)


def shard_levels(stream_key, extent, pieces, low, high):
    level = 1.0
    for position, shards_of in pieces:
        steps = jax.random.uniform(jax.random.fold_in(jax.random.fold_in(stream_key, 6), position), (shards_of,), jnp.float32, low / len(pieces), high / len(pieces))
        level = level * jnp.repeat(jnp.exp(steps), extent[position] // shards_of).reshape((-1,) + (1,) * (len(extent) - 1 - position))
    return level


def centred(own_key, extent, deviation, limit, shards=(), held_as=jnp.bfloat16):
    entries = deviation * jax.random.normal(own_key, extent, jnp.float32)
    if shards:
        entries = entries * shard_levels(own_key, extent, shards, -0.22, 0.18)
    return jnp.clip(entries, -limit, limit).astype(held_as)


def setup_inputs(seed: int = 0) -> dict:
    splits = jax.random.split(jax.random.key(seed), 8)
    return {
        "tokens": centred(splits[0], (BATCH, SPAN, D), 1.0, 6.0, ((0, 4), (2, 32))),
        "gain": jnp.clip(1.0 + 0.18 * jax.random.normal(splits[1], (D,), jnp.float32), 0.1, 1.9),
        "w_query": centred(splits[2], (D, QWIDTH), D ** -0.5, 0.046875, ((0, 4), (1, 32))),
        "w_keyval": centred(splits[3], (D, 2 * HEAD), (D // 4) ** -0.5, 0.09375, ((0, 4), (1, 32))),
        "w_out": centred(splits[4], (QWIDTH, D), HEAD ** -0.5, 0.375, ((0, 4), (1, 32))),
        "cache": draw_cache(jax.random.fold_in(splits[7], 71), 0),
        "lengths": draw_lengths(jax.random.fold_in(splits[7], 71), 0),
    }


def layer_norm(tokens, gain):
    values = tokens.astype(jnp.float32)
    mean = lax.optimization_barrier(jnp.mean(values, axis=-1, keepdims=True))
    centered = values - mean
    spread = lax.optimization_barrier(jnp.mean(centered * centered, axis=-1, keepdims=True))
    return (centered * lax.rsqrt(spread + 1e-06) * gain).astype(jnp.bfloat16)

def rotate(values, positions):
    width = values.shape[-1]
    half = width // 2
    freq = jnp.exp(jnp.arange(half, dtype=jnp.float32) * (-2.0 * math.log(10000.0) / width))
    angles = positions.astype(jnp.float32)[..., None] * freq
    cosine = jnp.cos(angles)[:, :, None, :]
    sine = jnp.sin(angles)[:, :, None, :]
    first = values[..., :half]
    second = values[..., half:]
    return jnp.concatenate([first * cosine - second * sine, second * cosine + first * sine], axis=-1)

def reference(tokens, gain, w_query, w_keyval, w_out, cache, lengths):
    normed = layer_norm(tokens, gain)
    flat = normed.reshape(BATCH * SPAN, D)
    positions = lengths[:, None] + jnp.arange(SPAN, dtype=jnp.int32)[None, :]
    query_raw = jnp.dot(flat, w_query, preferred_element_type=jnp.float32).reshape(BATCH, SPAN, HEADS, HEAD)
    query = rotate(query_raw, positions).astype(jnp.bfloat16)
    keyval = jnp.dot(flat, w_keyval, preferred_element_type=jnp.float32).astype(jnp.bfloat16).reshape(BATCH, SPAN, 2 * HEAD)
    fresh_keys = rotate(keyval[:, :, None, :HEAD].astype(jnp.float32), positions)[:, :, 0, :].astype(jnp.bfloat16)
    fresh_values = keyval[:, :, HEAD:]
    keys_all = jnp.concatenate([cache[:, :, :HEAD], fresh_keys], axis=1)
    values_all = jnp.concatenate([cache[:, :, HEAD:], fresh_values], axis=1)
    slots = jnp.arange(CACHE + SPAN, dtype=jnp.int32)
    steps = jnp.arange(SPAN, dtype=jnp.int32)
    cached_ok = (slots[None, None, :] < lengths[:, None, None]) & (slots[None, None, :] < CACHE)
    fresh_ok = (slots[None, None, :] >= CACHE) & (slots[None, None, :] - CACHE <= steps[None, :, None])
    valid = cached_ok | fresh_ok
    scale = 1.0 / math.sqrt(HEAD)

    def one_head(index):
        row = index // HEADS
        which = index % HEADS
        asked = query[row][:, which, :]
        scores = jnp.dot(asked, keys_all[row].T, preferred_element_type=jnp.float32) * scale
        mask = valid[row]
        largest = lax.optimization_barrier(jnp.max(jnp.where(mask, scores, -1e+30), axis=-1, keepdims=True))
        probs = jnp.exp(jnp.where(mask, scores - largest, -jnp.inf))
        total = lax.optimization_barrier(jnp.sum(probs, axis=-1, keepdims=True))
        summed = jnp.dot(probs.astype(jnp.bfloat16), values_all[row], preferred_element_type=jnp.float32)
        return (summed / total).astype(jnp.bfloat16)
    outputs = lax.map(one_head, jnp.arange(BATCH * HEADS, dtype=jnp.int32))
    outputs = outputs.reshape(BATCH, HEADS, SPAN, HEAD).transpose(0, 2, 1, 3).reshape(BATCH * SPAN, QWIDTH)
    attended = jnp.dot(outputs, w_out, preferred_element_type=jnp.float32).astype(jnp.bfloat16)
    return attended.reshape(BATCH, SPAN, D)
```

```python
import functools
import math

import jax
import jax.numpy as jnp
from jax import lax
from jax.experimental import pallas as pl
from jax.experimental.pallas import tpu as pltpu
from jax.sharding import PartitionSpec as P

MESH = pl.DeviceIdType.MESH
HEAD = 256
F32 = jnp.float32
BF16 = jnp.bfloat16


class Wires:
    def __init__(self, send, recv):
        self.send, self.recv, self.used, self.all = send, recv, 0, []

    def __call__(self, src, dst, target):
        k = self.used
        self.used += 1
        copy = pltpu.make_async_remote_copy(
            src_ref=src, dst_ref=dst, send_sem=self.send.at[k], recv_sem=self.recv.at[k],
            device_id=target, device_id_type=MESH,
        )
        copy.start()
        self.all.append(copy)
        return copy


def gather_plane(wires, unit, here, peer_y, peer_z, y, z, on_a, on_b):
    near = lambda v, d: lax.rem(v + d + 4, 4)
    yj = [y, near(y, -1), near(y, 1), near(y, 2)]
    zj = [z, near(z, -1), near(z, 1), near(z, 2)]

    def a(zz, yy, first=0, count=2):
        return unit(zz, yy, first, count)

    def b(zz, yy, first=2, count=2):
        return unit(zz, yy, first, count)

    def send(ref, target):
        return wires(ref, ref, target)

    zp, zm, yp, ym = [None] * 4, [None] * 4, [None] * 4, [None] * 4
    zfp, zfm, yfp, yfm = [None] * 4, [None] * 4, [None] * 4, [None] * 4

    def spread_a(j):
        zp[j] = send(a(z, yj[j]), peer_z(1))
        zm[j] = send(a(z, yj[j]), peer_z(-1))

    def spread_b(j):
        yp[j] = send(b(zj[j], y), peer_y(1))
        ym[j] = send(b(zj[j], y), peer_y(-1))

    def pass_a(j):
        zp[j].wait_recv()
        zfp[j] = send(a(zj[1], yj[j], 0, 1), peer_z(1))
        zm[j].wait_recv()
        zfm[j] = send(a(zj[2], yj[j], 1, 1), peer_z(-1))

    def pass_b(j):
        yp[j].wait_recv()
        yfp[j] = send(b(zj[j], yj[1], 2, 1), peer_y(1))
        ym[j].wait_recv()
        yfm[j] = send(b(zj[j], yj[2], 3, 1), peer_y(-1))

    a1p = send(a(z, y), peer_y(1))
    b1p = send(b(z, y), peer_z(1))
    a1m = send(a(z, y), peer_y(-1))
    b1m = send(b(z, y), peer_z(-1))
    spread_a(0)
    spread_b(0)
    a1p.wait_recv()
    a2p = send(a(z, yj[1], 0, 1), peer_y(1))
    spread_a(1)
    b1p.wait_recv()
    b2p = send(b(zj[1], y, 2, 1), peer_z(1))
    spread_b(1)
    a1m.wait_recv()
    a2m = send(a(z, yj[2], 1, 1), peer_y(-1))
    spread_a(2)
    b1m.wait_recv()
    b2m = send(b(zj[2], y, 3, 1), peer_z(-1))
    spread_b(2)
    pass_a(0)
    pass_b(0)
    a2p.wait_recv()
    a2m.wait_recv()
    spread_a(3)
    b2p.wait_recv()
    b2m.wait_recv()
    spread_b(3)
    for j in range(1, 4):
        pass_a(j)
        pass_b(j)
        zfp[j - 1].wait_recv()
        zfm[j - 1].wait_recv()
        yfp[j - 1].wait_recv()
        yfm[j - 1].wait_recv()
    for last in (zfp[3], zfm[3], yfp[3], yfm[3]):
        last.wait_recv()


def kernel(
    tokens, gain, w_query, w_keyval, w_out, cache, lengths, cos, sin, cos_t, sin_t, out,
    raw, stats, normed, whole, wq, kv_pair, wo, partial, q_send, kv_part, kv_send, q_recv, kv_recv,
    kv_t, slots, scores, weights, queries, totals, heads, heads_z, heads_all, o_send, o_recv,
    send_sem, recv_sem, local_sem,
):
    x = lax.axis_index("gx")
    yz = lax.axis_index("yz")
    z, y, c = yz // 8, (yz // 2) % 4, yz % 2
    near = lambda v, d: lax.rem(v + d + 4, 4)

    def device(xx, zz, yy, cc):
        return (xx, zz * 8 + yy * 2 + cc)

    peer_x = lambda d, dc=0: device(near(x, d), z, y, lax.rem(c + dc, 2))
    peer_y = lambda d: device(x, z, near(y, d), c)
    peer_z = lambda d, dc=0: device(x, near(z, d), y, lax.rem(c + dc, 2))
    sibling = device(x, z, y, 1 - c)

    barrier = pltpu.get_barrier_semaphore()
    peers = [sibling]
    for d in (1, 2, 3):
        peers += [peer_x(d), peer_x(d, 1), peer_z(d), peer_z(d, 1), peer_y(d)]
    for p in peers:
        pl.semaphore_signal(barrier, inc=1, device_id=p, device_id_type=MESH)

    locals_ = []

    def local(src, dst):
        copy = pltpu.make_async_copy(src, dst, local_sem.at[len(locals_)])
        copy.start()
        locals_.append(copy)
        return copy

    own_raw = local(tokens.at[0, pl.ds(pl.multiple_of(c * 128 + z * 32, 32), 32), :], raw.at[z, c])
    own_wq = local(w_query, wq.at[:, pl.ds(pl.multiple_of(c * 256, 256), 256)])
    own_kv = local(w_keyval, kv_pair.at[c])
    own_wo = local(w_out, wo.at[c])
    own_slots = local(cache.at[0], slots.at[pl.ds(pl.multiple_of(yz * 64, 64), 64), :])

    pl.semaphore_wait(barrier, len(peers))
    wires = Wires(send_sem, recv_sem)

    first = []
    for d in (0, 1, 2, 3):
        for dc in (0, 1):
            if d or dc:
                zz, cc = near(z, d), lax.rem(c + dc, 2)
                rows = pl.ds(pl.multiple_of(cc * 128 + zz * 32, 32), 32)
                first.append(wires(tokens.at[0, rows, :], raw.at[z, c], device(x, zz, y, cc)))
    slot_rows = lambda zz, yy: slots.at[pl.ds(pl.multiple_of((zz * 8 + yy * 2 + c) * 64, 64), 64), :]
    own_slots.wait()
    cache_y = [wires(slot_rows(z, y), slot_rows(z, y), peer_y(d)) for d in (1, 2, 3)]
    wq_copy = wires(w_query, wq.at[:, pl.ds(pl.multiple_of(c * 256, 256), 256)], sibling)
    kv_copy = wires(w_keyval, kv_pair.at[c], sibling)
    wo_copy = wires(w_out, wo.at[c], sibling)

    own_raw.wait()
    for copy in first:
        copy.wait_recv()
    values = raw[...].astype(F32)
    mean = jnp.sum(jnp.sum(values, axis=(0, 1)), axis=-1, keepdims=True) * (1.0 / 4608)
    centered = values - mean[None, None]
    square = jnp.sum(jnp.sum(centered * centered, axis=(0, 1)), axis=-1, keepdims=True)
    lane = lax.broadcasted_iota(jnp.int32, (32, 128), 1)
    stats[y] = jnp.where(lane < 64, mean, square)
    stat_copies = [wires(stats.at[y], stats.at[y], peer_y(d)) for d in (1, 2, 3)]
    for copy in stat_copies:
        copy.wait_recv()
    means = [stats[k][:, 0:1] for k in range(4)]
    squares = [stats[k][:, 64:65] for k in range(4)]
    mean = (means[0] + means[1] + means[2] + means[3]) * 0.25
    spread = squares[0] + squares[1] + squares[2] + squares[3]
    for k in range(4):
        spread = spread + 4608.0 * (means[k] - mean) * (means[k] - mean)
    scale = lax.rsqrt(spread * (1.0 / 18432) + 1e-6)
    for i in range(4):
        both = []
        for k in range(2):
            g = gain[pl.ds(i * 8 + y * 2 + k, 1), :]
            both.append((raw[i, k].astype(F32) - mean) * scale * g)
        normed[i] = jnp.concatenate(both, axis=-1).astype(BF16)

    def unit(zz, yy, start, count):
        return whole.at[
            pl.ds(pl.multiple_of(zz * 128 + start * 32, 32), count * 32),
            pl.ds(pl.multiple_of(yy * 1152, 128), 1152),
        ]

    mine = local(normed.at[x], unit(z, y, x, 1))
    second = [wires(normed.at[near(x, d)], unit(z, y, x, 1), peer_x(d)) for d in (1, 3, 2)]
    for copy in cache_y:
        copy.wait_recv()
    cache_z = []
    for k in range(4):
        cache_z.append(wires(slot_rows(z, k), slot_rows(z, k), sibling))
    for d in (1, 3, 2):
        for k in range(4):
            for dc in (0, 1):
                cache_z.append(wires(slot_rows(z, k), slot_rows(z, k), peer_z(d, dc)))
    mine.wait()
    for copy in second:
        copy.wait_recv()
    gather_plane(wires, unit, None, peer_y, peer_z, y, z, None, None)

    for copy in (own_wq, own_kv, own_wo):
        copy.wait()
    for copy in (wq_copy, kv_copy):
        copy.wait_recv()

    @pl.loop(0, 18)
    def _(s):
        rows = pl.ds(pl.multiple_of(s * 256, 256), 256)
        pair = jnp.concatenate(
            [kv_pair[0, rows, :].astype(F32), kv_pair[1, rows, :].astype(F32), jnp.zeros((256, 96), F32)], axis=-1
        )
        wq[rows, 512:640] = pair.astype(BF16)

    @pl.loop(0, 4)
    def _(r):
        rows = pl.ds(pl.multiple_of(r * 128, 128), 128)
        acc = jnp.dot(whole[rows, :], wq[...], preferred_element_type=F32)
        partial[r] = acc[:, :512]
        q_send[r] = acc[:, :512].astype(BF16)
        kv_part[r] = acc[:, 512:]

    for b in range(4):
        block = jnp.concatenate([kv_part[r, b * 32:(b + 1) * 32, :] for r in range(4)], axis=0)
        kv_send[b] = block.T[:32, :]
    thirds = []
    for d in (1, 3, 2):
        xx = near(x, d)
        thirds.append(wires(kv_send.at[xx], kv_recv.at[x], peer_x(d)))
    for d in (1, 3, 2):
        rows = pl.ds(pl.multiple_of(near(x, d) * 32, 32), 32)
        thirds.append(wires(q_send.at[:, rows, :], q_recv.at[x], peer_x(d)))
    for copy in thirds[:3]:
        copy.wait_recv()
    total = kv_send[x]
    for d in (1, 2, 3):
        total = total + kv_recv[near(x, d)]
    kv_block = lambda zz, yy: kv_t.at[
        pl.ds(pl.multiple_of((zz * 4 + yy) * 32, 32), 32), pl.ds(pl.multiple_of(c * 128, 128), 128)
    ]
    kv_t[pl.ds(pl.multiple_of((z * 4 + y) * 32, 32), 32), pl.ds(pl.multiple_of(c * 128, 128), 128)] = total.astype(BF16)
    kv_y = [wires(kv_block(z, y), kv_block(z, y), peer_y(d)) for d in (1, 2, 3)]
    for copy in kv_y:
        copy.wait_recv()
    kv_rows = kv_t.at[pl.ds(pl.multiple_of(z * 128, 128), 128), pl.ds(pl.multiple_of(c * 128, 128), 128)]
    kv_z = [wires(kv_rows, kv_rows, sibling)]
    for d in (1, 3, 2):
        for dc in (0, 1):
            kv_z.append(wires(kv_rows, kv_rows, peer_z(d, dc)))

    for copy in thirds[3:]:
        copy.wait_recv()
    mine_rows = pl.ds(pl.multiple_of(x * 32, 32), 32)
    query = partial[:, mine_rows, :].reshape(128, 512)
    for d in (1, 2, 3):
        query = query + q_recv[near(x, d)].reshape(128, 512).astype(F32)
    half_rows = pl.ds(pl.multiple_of(c * 128, 128), 128)
    cosine, sine = cos[half_rows, :], sin[half_rows, :]
    for h in range(2):
        u, w = query[:, h * 256:h * 256 + 128], query[:, h * 256 + 128:h * 256 + 256]
        queries[h * 128:(h + 1) * 128, 0:128] = (u * cosine - w * sine).astype(BF16)
        queries[h * 128:(h + 1) * 128, 128:256] = (w * cosine + u * sine).astype(BF16)
    for copy in cache_z:
        copy.wait_recv()
    inv = 1.0 / math.sqrt(HEAD)
    contract = (((1,), (1,)), ((), ()))

    @pl.loop(0, 8)
    def _(k):
        at = pl.ds(pl.multiple_of(k * 256, 256), 256)
        s = lax.dot_general(queries[...], slots[at, 0:256], contract, preferred_element_type=F32) * inv
        col = k * 256 + lax.broadcasted_iota(jnp.int32, (256, 256), 1)
        scores[:, at] = jnp.where(col < lengths[0], s, -1e30)

    for copy in kv_z:
        copy.wait_recv()
    u, w = kv_t[0:128, :].astype(F32), kv_t[128:256, :].astype(F32)
    ct, st = cos_t[...], sin_t[...]
    fresh = jnp.concatenate([u * ct - w * st, w * ct + u * st], axis=0).astype(BF16)
    s = jnp.dot(queries[...], fresh, preferred_element_type=F32) * inv
    t = c * 128 + lax.rem(lax.broadcasted_iota(jnp.int32, (256, 256), 0), 128)
    t2 = lax.broadcasted_iota(jnp.int32, (256, 256), 1)
    scores[:, 2048:2304] = jnp.where(t2 <= t, s, -1e30)

    @pl.loop(0, 8)
    def _(k):
        at = pl.ds(pl.multiple_of(k * 32, 32), 32)
        s = scores[at, :]
        p = jnp.exp(s - jnp.max(s, axis=-1, keepdims=True))
        totals[at, :] = jnp.broadcast_to(jnp.sum(p, axis=-1, keepdims=True), (32, 128))
        weights[at, :] = p.astype(BF16)

    for h in range(2):
        at = slice(h * 128, (h + 1) * 128)
        summed = jnp.dot(weights[at, 0:2048], slots[:, 256:512], preferred_element_type=F32)
        summed += lax.dot_general(weights[at, 2048:2304], kv_t[256:512, :], contract, preferred_element_type=F32)
        heads[:, h * 256:(h + 1) * 256] = (summed / totals[at, 0:1]).astype(BF16)

    fourth = []
    for d in (1, 3, 2):
        rows = pl.ds(pl.multiple_of(near(z, d) * 32, 32), 32)
        fourth.append(wires(heads.at[rows, :], heads_z.at[z], peer_z(d)))
    own = local(heads.at[pl.ds(pl.multiple_of(z * 32, 32), 32), :], heads_z.at[z])

    def head_unit(zz, yy, start, count):
        return heads_all.at[
            pl.ds(pl.multiple_of(zz * 128 + start * 32, 32), count * 32),
            pl.ds(pl.multiple_of(yy * 512, 128), 512),
        ]

    own.wait()
    for copy in fourth:
        copy.wait_recv()
    mine = local(heads_z.at[x], head_unit(z, y, x, 1))
    fifth = [wires(heads_z.at[near(x, d)], head_unit(z, y, x, 1), peer_x(d)) for d in (1, 3, 2)]
    mine.wait()
    for copy in fifth:
        copy.wait_recv()
    gather_plane(wires, head_unit, None, peer_y, peer_z, y, z, None, None)

    wo_copy.wait_recv()
    last = []
    for r in range(4):
        for k in range(2):
            o_send[k, r] = jnp.dot(
                heads_all[r * 128:(r + 1) * 128, :], wo[k], preferred_element_type=F32
            ).astype(BF16)
    for d in (1, 3, 2, 0):
        rows = pl.ds(pl.multiple_of(near(x, d) * 32, 32), 32)
        for dc in (0, 1):
            if d or dc:
                cc = lax.rem(c + dc, 2)
                last.append(wires(o_send.at[cc, :, rows, :], o_recv.at[x, c], peer_x(d, dc)))
    own = local(o_send.at[c, :, pl.ds(pl.multiple_of(x * 32, 32), 32), :], o_recv.at[x, c])
    own.wait()
    for copy in last:
        copy.wait_recv()
    for k in range(2):
        total = o_recv[0, k].astype(F32)
        for xx in (1, 2, 3):
            total = total + o_recv[xx, k].astype(F32)
        out[0, k * 128:(k + 1) * 128, :] = total.reshape(128, 576).astype(BF16)

    for copy in wires.all:
        copy.wait_send()


def tables(lengths):
    half = HEAD // 2
    freq = jnp.exp(jnp.arange(half, dtype=F32) * (-2.0 * math.log(10000.0) / HEAD))
    positions = (lengths[0] + jnp.arange(256, dtype=jnp.int32)).astype(F32)
    angles = positions[:, None] * freq[None, :]
    angles_t = freq[:, None] * positions[None, :]
    return jnp.cos(angles), jnp.sin(angles), jnp.cos(angles_t), jnp.sin(angles_t)


def body(tokens, gain, w_query, w_keyval, w_out, cache, lengths):
    hbm = pl.BlockSpec(memory_space=pl.ANY)
    vmem = pl.BlockSpec(memory_space=pltpu.VMEM)
    smem = pl.BlockSpec(memory_space=pltpu.SMEM)
    return pl.pallas_call(
        kernel,
        out_shape=jax.ShapeDtypeStruct((1, 256, 576), BF16),
        in_specs=[hbm, vmem, hbm, hbm, hbm, hbm, smem, vmem, vmem, vmem, vmem],
        out_specs=vmem,
        scratch_shapes=[
            pltpu.VMEM((4, 2, 32, 576), BF16),
            pltpu.VMEM((4, 32, 128), F32),
            pltpu.VMEM((4, 32, 1152), BF16),
            pltpu.VMEM((512, 4608), BF16),
            pltpu.VMEM((4608, 640), BF16),
            pltpu.VMEM((2, 4608, 16), BF16),
            pltpu.VMEM((2, 2048, 576), BF16),
            pltpu.VMEM((4, 128, 512), F32),
            pltpu.VMEM((4, 128, 512), BF16),
            pltpu.VMEM((4, 128, 128), F32),
            pltpu.VMEM((4, 32, 128), F32),
            pltpu.VMEM((4, 4, 32, 512), BF16),
            pltpu.VMEM((4, 32, 128), F32),
            pltpu.VMEM((512, 256), BF16),
            pltpu.VMEM((2048, 512), BF16),
            pltpu.VMEM((256, 2304), F32),
            pltpu.VMEM((256, 2304), BF16),
            pltpu.VMEM((256, 256), BF16),
            pltpu.VMEM((256, 128), F32),
            pltpu.VMEM((128, 512), BF16),
            pltpu.VMEM((4, 32, 512), BF16),
            pltpu.VMEM((512, 2048), BF16),
            pltpu.VMEM((2, 4, 128, 576), BF16),
            pltpu.VMEM((4, 2, 4, 32, 576), BF16),
            pltpu.SemaphoreType.DMA((176,)),
            pltpu.SemaphoreType.DMA((176,)),
            pltpu.SemaphoreType.DMA((16,)),
        ],
        compiler_params=pltpu.CompilerParams(
            collective_id=0, has_side_effects=True, vmem_limit_bytes=56 * 1024 * 1024
        ),
    )(
        tokens, gain.reshape(32, 576), w_query, w_keyval, w_out, cache, lengths, *tables(lengths)
    )


def solution(mesh):
    return jax.shard_map(
        body,
        mesh=mesh,
        in_specs=(
            P("gx", None, "yz"),
            P(),
            P("gx", "yz"),
            P("gx", "yz"),
            P("gx", "yz"),
            P("gx", "yz", None),
            P("gx"),
        ),
        out_specs=P("gx", None, "yz"),
        check_vma=False,
    )
```

```python
import math

import jax
import jax.numpy as jnp
from jax import lax
from jax.experimental import pallas as pl
from jax.experimental.pallas import tpu as pltpu
from jax.sharding import PartitionSpec as P

MESH = pl.DeviceIdType.MESH
HEAD = 256
F32 = jnp.float32
BF16 = jnp.bfloat16
LEFT = (((0,), (0,)), ((), ()))


class Wires:
    def __init__(self, send, recv):
        self.send, self.recv, self.used, self.all = send, recv, 0, []

    def __call__(self, src, dst, target):
        k = self.used
        self.used += 1
        copy = pltpu.make_async_remote_copy(
            src_ref=src, dst_ref=dst, send_sem=self.send.at[k], recv_sem=self.recv.at[k],
            device_id=target, device_id_type=MESH,
        )
        copy.start()
        self.all.append(copy)
        return copy


def near(v, d):
    return lax.rem(v + d + 4, 4)


def gather_plane(wires, unit, peer_y, peer_z, y, z, on_a=lambda j: None):
    yj = [y, near(y, -1), near(y, 1), near(y, 2)]
    zj = [z, near(z, -1), near(z, 1), near(z, 2)]

    def send(ref, target):
        return wires(ref, ref, target)

    zp, zm, yp, ym = [None] * 4, [None] * 4, [None] * 4, [None] * 4
    zfp, zfm, yfp, yfm = [None] * 4, [None] * 4, [None] * 4, [None] * 4

    def spread_a(j):
        zp[j] = send(unit(z, yj[j], 0, 2), peer_z(1))
        zm[j] = send(unit(z, yj[j], 0, 2), peer_z(-1))

    def spread_b(j):
        yp[j] = send(unit(zj[j], y, 2, 2), peer_y(1))
        ym[j] = send(unit(zj[j], y, 2, 2), peer_y(-1))

    def pass_a(j):
        zp[j].wait_recv()
        zfp[j] = send(unit(zj[1], yj[j], 0, 1), peer_z(1))
        zm[j].wait_recv()
        zfm[j] = send(unit(zj[2], yj[j], 1, 1), peer_z(-1))

    def pass_b(j):
        yp[j].wait_recv()
        yfp[j] = send(unit(zj[j], yj[1], 2, 1), peer_y(1))
        ym[j].wait_recv()
        yfm[j] = send(unit(zj[j], yj[2], 3, 1), peer_y(-1))

    a1p = send(unit(z, y, 0, 2), peer_y(1))
    b1p = send(unit(z, y, 2, 2), peer_z(1))
    a1m = send(unit(z, y, 0, 2), peer_y(-1))
    b1m = send(unit(z, y, 2, 2), peer_z(-1))
    spread_a(0)
    spread_b(0)
    yield
    a1p.wait_recv()
    a2p = send(unit(z, yj[1], 0, 1), peer_y(1))
    spread_a(1)
    b1p.wait_recv()
    b2p = send(unit(zj[1], y, 2, 1), peer_z(1))
    spread_b(1)
    yield
    a1m.wait_recv()
    a2m = send(unit(z, yj[2], 1, 1), peer_y(-1))
    spread_a(2)
    b1m.wait_recv()
    b2m = send(unit(zj[2], y, 3, 1), peer_z(-1))
    spread_b(2)
    yield
    pass_a(0)
    pass_b(0)
    yield
    a2p.wait_recv()
    a2m.wait_recv()
    spread_a(3)
    b2p.wait_recv()
    b2m.wait_recv()
    spread_b(3)
    yield
    for j in range(1, 4):
        pass_a(j)
        pass_b(j)
        zfp[j - 1].wait_recv()
        zfm[j - 1].wait_recv()
        on_a(j - 1)
        yield
    for copy in (zfp[3], zfm[3]):
        copy.wait_recv()
    on_a(3)
    for j in range(4):
        yfp[j].wait_recv()
        yfm[j].wait_recv()


def kernel(
    tokens, gain, w_query, w_keyval, w_out, cache, lengths, out,
    mine, raw, stat_y, stat_z, gain_col, normed, whole, w_rows, w_t, wo, acc, q_send, q_recv, kv_send, kv_recv,
    kv_t, keys, values, values_t, cosine, sine, scores, weights, queries, heads, heads_z, heads_all, acc_o, o_send, o_recv,
    send_sem, recv_sem, local_sem,
):
    x = lax.axis_index("gx")
    yz = lax.axis_index("yz")
    z, y, c = yz // 8, (yz // 2) % 4, yz % 2

    def device(xx, zz, yy, cc):
        return (xx, zz * 8 + yy * 2 + cc)

    peer_x = lambda d, dc=0: device(near(x, d), z, y, lax.rem(c + dc, 2))
    peer_y = lambda d: device(x, z, near(y, d), c)
    peer_z = lambda d, dc=0: device(x, near(z, d), y, lax.rem(c + dc, 2))
    sibling = device(x, z, y, 1 - c)

    barrier = pltpu.get_barrier_semaphore()
    peers = [sibling]
    for d in (1, 2, 3):
        peers += [peer_x(d), peer_x(d, 1), peer_z(d), peer_z(d, 1), peer_y(d)]
    for p in peers:
        pl.semaphore_signal(barrier, inc=1, device_id=p, device_id_type=MESH)

    locals_ = []

    def local(src, dst):
        copy = pltpu.make_async_copy(src, dst, local_sem.at[len(locals_)])
        copy.start()
        locals_.append(copy)
        return copy

    quarter = lambda k: pl.ds(pl.multiple_of(k * 144, 16), 144)
    own_mine = local(tokens.at[0], mine)
    slot_rows = pl.ds(pl.multiple_of(yz * 64, 64), 64)
    own_keys = local(cache.at[0, :, 0:256], keys.at[slot_rows, :])
    own_values = local(cache.at[0, :, 256:512], values.at[slot_rows, :])
    own_raw = local(tokens.at[0, quarter(z), :], raw.at[z])
    own_rows = local(w_query, w_rows)
    kv_rows16 = pl.ds(pl.multiple_of(512 + c * 16, 16), 16)
    own_kv = local(w_keyval, w_t.at[kv_rows16, :])
    own_wo = local(w_out, wo.at[c])

    own_mine.wait()
    v = mine[...].astype(F32)
    mean = jnp.sum(v, axis=0, keepdims=True) * (1.0 / 576)
    square = jnp.sum((v - mean) * (v - mean), axis=0, keepdims=True)
    row = lax.broadcasted_iota(jnp.int32, (8, 256), 0)

    def join(ref, count, size):
        means = [ref[k][0:1] for k in range(count)]
        mid = sum(means[1:], means[0]) * (1.0 / count)
        total = sum([ref[k][1:2] for k in range(1, count)], ref[0][1:2])
        for m in means:
            total = total + size * (m - mid) * (m - mid)
        return mid, total

    stat_y[y] = jnp.where(row == 0, mean, square)
    pl.semaphore_wait(barrier, len(peers))
    wires = Wires(send_sem, recv_sem)
    stat_1 = [wires(stat_y.at[y], stat_y.at[y], peer_y(d)) for d in (1, 3, 2)]
    first = [wires(tokens.at[0, quarter(near(z, d)), :], raw.at[z], peer_z(d)) for d in (1, 3, 2)]
    own_keys.wait()
    own_values.wait()

    def cache_unit(zz, yy, start, count):
        at = pl.ds(pl.multiple_of((zz * 8 + yy * 2 + c) * 64 + (start % 2) * 32, 32), count * 32)
        return keys.at[at, :] if start < 2 else values.at[at, :]

    cached = gather_plane(wires, cache_unit, peer_y, peer_z, y, z)
    next(cached)

    lane = lax.broadcasted_iota(jnp.int32, (16, 128), 1)
    sub = lax.broadcasted_iota(jnp.int32, (16, 128), 0)

    @pl.loop(0, 36)
    def _(k):
        g = (k // 9) * 288 + y * 72 + c * 36 + z * 9 + k % 9
        line = jnp.broadcast_to(gain[pl.ds(g // 8, 1), :], (16, 128))
        col = jnp.sum(jnp.where(lane == sub + (g % 8) * 16, line, 0.0), axis=1, keepdims=True)
        gain_col[pl.ds(pl.multiple_of(k * 16, 16), 16), :] = jnp.broadcast_to(col, (16, 256))

    for copy in stat_1:
        copy.wait_recv()
    mean, square = join(stat_y, 4, 576.0)
    me = z * 2 + c
    stat_z[me] = jnp.where(row == 0, mean, square)
    stat_2 = [wires(stat_z.at[me], stat_z.at[me], sibling)]
    for d in (1, 3, 2):
        for dc in (0, 1):
            stat_2.append(wires(stat_z.at[me], stat_z.at[me], peer_z(d, dc)))
    for copy in stat_2:
        copy.wait_recv()
    mean, square = join(stat_z, 8, 2304.0)
    scale = lax.rsqrt(square * (1.0 / 18432) + 1e-6)
    own_raw.wait()
    for copy in first:
        copy.wait_recv()
    for i in range(4):
        n = ((raw[i].astype(F32) - mean) * scale * gain_col[i * 144:(i + 1) * 144, :]).astype(BF16)
        for k in range(2):
            normed[i, k] = n[:, k * 128:(k + 1) * 128]

    spot = whole.at[x // 2, y, x % 2, c, z]
    second = []
    for d in (1, 3, 2, 0):
        for dc in (0, 1):
            if d or dc:
                second.append(wires(normed.at[near(x, d), lax.rem(c + dc, 2)], spot, peer_x(d, dc)))
    own_spot = local(normed.at[x, c], spot)
    next(cached)
    next(cached)
    next(cached)
    own_spot.wait()
    for copy in second:
        copy.wait_recv()

    def unit(zz, yy, start, count):
        if count == 2:
            return whole.at[start // 2, yy, :, :, zz]
        return whole.at[start // 2, yy, start % 2, :, zz]

    def project(half, yy, fresh_start):
        right = jnp.concatenate([whole[half, yy, b].reshape(1152, 128) for b in range(2)], axis=1)
        left = w_t[:, pl.ds(pl.multiple_of(yy * 1152, 128), 1152)]
        part = jnp.dot(left, right, preferred_element_type=F32)
        if fresh_start:
            acc[half] = part
        else:
            acc[half] += part

    yj = [y, near(y, -1), near(y, 1), near(y, 2)]
    gathered = gather_plane(wires, unit, peer_y, peer_z, y, z, lambda j: project(0, yj[j], j == 0))
    next(gathered)
    own_rows.wait()
    w_mine = pl.ds(pl.multiple_of(c * 256, 256), 256)

    @pl.loop(0, 18)
    def _(s):
        at = pl.ds(pl.multiple_of(s * 256, 256), 256)
        w_t[w_mine, at] = w_rows[at, :].T

    own_kv.wait()
    own_wo.wait()
    shared = [
        wires(w_t.at[w_mine, :], w_t.at[w_mine, :], sibling),
        wires(w_keyval, w_t.at[kv_rows16, :], sibling),
        wires(w_out, wo.at[c], sibling),
    ]
    next(gathered)
    next(gathered)
    for _ in cached:
        pass
    next(gathered)
    pair_rows = lambda ref: ref.reshape(16, 2, 64, 256).at[:, c]
    share_keys = wires(pair_rows(keys), pair_rows(keys), sibling)
    share_values = wires(pair_rows(values), pair_rows(values), sibling)
    freq = jnp.exp(
        lax.broadcasted_iota(jnp.int32, (128, 256), 0).astype(F32) * (-2.0 * math.log(10000.0) / HEAD)
    )
    angle = (lengths[0] + lax.broadcasted_iota(jnp.int32, (128, 256), 1)).astype(F32) * freq
    cosine[...] = jnp.cos(angle)
    sine[...] = jnp.sin(angle)
    for copy in shared[:2]:
        copy.wait_recv()
    for _ in gathered:
        pass

    @pl.loop(0, 4)
    def _(k):
        right = jnp.concatenate([whole[1, k, b].reshape(1152, 128) for b in range(2)], axis=1)
        left = w_t[:, pl.ds(pl.multiple_of(k * 1152, 128), 1152)]
        part = jnp.dot(left, right, preferred_element_type=F32)

        @pl.when(k == 0)
        def _():
            acc[1] = part

        @pl.when(k > 0)
        def _():
            acc[1] += part

    for b in range(4):
        lanes = slice((b % 2) * 128, (b % 2) * 128 + 128)
        kv_send[b] = acc[b // 2, 512:544, lanes]
        q_send[b] = acc[b // 2, 0:512, lanes].astype(BF16)
    third, fourth = [], []
    for d in (1, 3, 2):
        third.append(wires(kv_send.at[near(x, d)], kv_recv.at[x], peer_x(d)))
    for d in (1, 3, 2):
        fourth.append(wires(q_send.at[near(x, d)], q_recv.at[x], peer_x(d)))
    for copy in third:
        copy.wait_recv()
    total = kv_send[x]
    for d in (1, 2, 3):
        total = total + kv_recv[near(x, d)]
    kv_block = lambda zz, yy: kv_t.at[c, pl.ds(pl.multiple_of((zz * 4 + yy) * 32, 32), 32), :]
    kv_t[c, pl.ds(pl.multiple_of((z * 4 + y) * 32, 32), 32), :] = total.astype(BF16)
    kv_y = [wires(kv_block(z, y), kv_block(z, y), peer_y(d)) for d in (1, 3, 2)]
    for copy in kv_y:
        copy.wait_recv()
    kv_rows = kv_t.at[c, pl.ds(pl.multiple_of(z * 128, 128), 128), :]
    kv_z = [wires(kv_rows, kv_rows, sibling)]
    for d in (1, 3, 2):
        for dc in (0, 1):
            kv_z.append(wires(kv_rows, kv_rows, peer_z(d, dc)))
    share_values.wait_recv()

    @pl.loop(0, 8)
    def _(s):
        at = pl.ds(pl.multiple_of(s * 256, 256), 256)
        values_t[:, at] = values[at, :].T

    share_keys.wait_recv()

    for copy in fourth:
        copy.wait_recv()
    query = q_send[x].astype(F32)
    for d in (1, 2, 3):
        query = query + q_recv[near(x, d)].astype(F32)
    half_lanes = pl.ds(pl.multiple_of(c * 128, 128), 128)
    cos_q, sin_q = cosine[:, half_lanes], sine[:, half_lanes]
    for h in range(2):
        u, w = query[h * 256:h * 256 + 128], query[h * 256 + 128:h * 256 + 256]
        queries[0:128, h * 128:(h + 1) * 128] = (u * cos_q - w * sin_q).astype(BF16)
        queries[128:256, h * 128:(h + 1) * 128] = (w * cos_q + u * sin_q).astype(BF16)
    inv = 1.0 / math.sqrt(HEAD)

    def fold(s, f):
        return f(s.reshape(s.shape[0] // 8, 8, 256), axis=0)

    def cached_scores(k, top):
        at = pl.ds(pl.multiple_of(k * 256, 256), 256)
        s = jnp.dot(keys[at, :], queries[...], preferred_element_type=F32) * inv
        slot = k * 256 + lax.broadcasted_iota(jnp.int32, (256, 256), 0)
        s = jnp.where(slot < lengths[0], s, -1e30)
        scores[at, :] = s
        return jnp.maximum(top, fold(s, jnp.max))

    top = lax.fori_loop(0, 8, cached_scores, jnp.full((8, 256), -1e30, F32))
    for copy in kv_z:
        copy.wait_recv()
    kv = jnp.concatenate([kv_t[0], kv_t[1]], axis=1)
    u, w = kv[0:128].astype(F32), kv[128:256].astype(F32)
    fresh = jnp.concatenate([u * cosine[...] - w * sine[...], w * cosine[...] + u * sine[...]], axis=0).astype(BF16)
    s = lax.dot_general(fresh, queries[...], LEFT, preferred_element_type=F32) * inv
    t = c * 128 + lax.rem(lax.broadcasted_iota(jnp.int32, (256, 256), 1), 128)
    t2 = lax.broadcasted_iota(jnp.int32, (256, 256), 0)
    s = jnp.where(t2 <= t, s, -1e30)
    scores[2048:2304, :] = s
    top = jnp.max(jnp.maximum(top, fold(s, jnp.max)), axis=0, keepdims=True)

    def exponentials(k, total):
        at = pl.ds(pl.multiple_of(k * 256, 256), 256)
        p = jnp.exp(scores[at, :] - top)
        weights[at, :] = p.astype(BF16)
        return total + fold(p, jnp.sum)

    total = jnp.sum(lax.fori_loop(0, 9, exponentials, jnp.zeros((8, 256), F32)), axis=0, keepdims=True)
    summed = jnp.dot(values_t[...], weights[0:2048, :], preferred_element_type=F32)
    summed += jnp.dot(kv[256:512], weights[2048:2304, :], preferred_element_type=F32)
    done = (summed / total).astype(BF16)
    heads[0] = done[:, 0:128]
    heads[1] = done[:, 128:256]

    fifth = []
    for d in (1, 3, 2):
        rows = pl.ds(pl.multiple_of(near(z, d) * 64, 64), 64)
        fifth.append(wires(heads.at[:, rows, :], heads_z.at[z], peer_z(d)))
    own = local(heads.at[:, pl.ds(pl.multiple_of(z * 64, 64), 64), :], heads_z.at[z])
    own.wait()
    for copy in fifth:
        copy.wait_recv()
    head_spot = heads_all.at[x // 2, y, x % 2, :, z]
    sixth = [wires(heads_z.at[near(x, d)], head_spot, peer_x(d)) for d in (1, 3, 2)]
    own = local(heads_z.at[x], head_spot)
    own.wait()
    for copy in sixth:
        copy.wait_recv()

    def head_unit(zz, yy, start, count):
        if count == 2:
            return heads_all.at[start // 2, yy, :, :, zz]
        return heads_all.at[start // 2, yy, start % 2, :, zz]

    shared[2].wait_recv()

    def project_out(half, yy, fresh_start):
        right = jnp.concatenate([heads_all[half, yy, b].reshape(512, 128) for b in range(2)], axis=1)
        for k in range(2):
            left = wo[k, :, pl.ds(pl.multiple_of(yy * 512, 128), 512)]
            part = jnp.dot(left, right, preferred_element_type=F32)
            if fresh_start:
                acc_o[k] = part
            else:
                acc_o[k] += part

    for _ in gather_plane(wires, head_unit, peer_y, peer_z, y, z, lambda j: project_out(0, yj[j], j == 0)):
        pass
    right = jnp.concatenate([heads_all[1, :, b].reshape(2048, 128) for b in range(2)], axis=1)
    for k in range(2):
        for b in range(2):
            o_send[b, k] = acc_o[k][:, b * 128:(b + 1) * 128].astype(BF16)
        part = jnp.dot(wo[k], right, preferred_element_type=F32)
        for b in range(2):
            o_send[2 + b, k] = part[:, b * 128:(b + 1) * 128].astype(BF16)
    last = []
    for d in (2, 1, 3, 0):
        for dc in (0, 1):
            if d or dc:
                last.append(wires(o_send.at[near(x, d), lax.rem(c + dc, 2)], o_recv.at[x, c], peer_x(d, dc)))
    own = local(o_send.at[x, c], o_recv.at[x, c])
    own.wait()
    for copy in last:
        copy.wait_recv()
    for k in range(2):
        total = o_recv[0, k].astype(F32)
        for xx in (1, 2, 3):
            total = total + o_recv[xx, k].astype(F32)
        out[0, :, k * 128:(k + 1) * 128] = total.astype(BF16)

    for copy in wires.all:
        copy.wait_send()


def body(tokens, gain, w_query, w_keyval, w_out, cache, lengths):
    hbm = pl.BlockSpec(memory_space=pl.ANY)
    vmem = pl.BlockSpec(memory_space=pltpu.VMEM)
    smem = pl.BlockSpec(memory_space=pltpu.SMEM)
    out = pl.pallas_call(
        kernel,
        out_shape=jax.ShapeDtypeStruct((1, 576, 256), BF16),
        in_specs=[hbm, vmem, hbm, hbm, hbm, hbm, smem],
        out_specs=vmem,
        scratch_shapes=[
            pltpu.VMEM((576, 256), BF16),
            pltpu.VMEM((4, 144, 256), BF16),
            pltpu.VMEM((4, 8, 256), F32),
            pltpu.VMEM((8, 8, 256), F32),
            pltpu.VMEM((576, 256), F32),
            pltpu.VMEM((4, 2, 144, 128), BF16),
            pltpu.VMEM((2, 4, 2, 2, 4, 144, 128), BF16),
            pltpu.VMEM((4608, 256), BF16),
            pltpu.VMEM((544, 4608), BF16),
            pltpu.VMEM((2, 576, 2048), BF16),
            pltpu.VMEM((2, 544, 256), F32),
            pltpu.VMEM((4, 512, 128), BF16),
            pltpu.VMEM((4, 512, 128), BF16),
            pltpu.VMEM((4, 32, 128), F32),
            pltpu.VMEM((4, 32, 128), F32),
            pltpu.VMEM((2, 512, 128), BF16),
            pltpu.VMEM((2048, 256), BF16),
            pltpu.VMEM((2048, 256), BF16),
            pltpu.VMEM((256, 2048), BF16),
            pltpu.VMEM((128, 256), F32),
            pltpu.VMEM((128, 256), F32),
            pltpu.VMEM((2304, 256), F32),
            pltpu.VMEM((2304, 256), BF16),
            pltpu.VMEM((256, 256), BF16),
            pltpu.VMEM((2, 256, 128), BF16),
            pltpu.VMEM((4, 2, 64, 128), BF16),
            pltpu.VMEM((2, 4, 2, 2, 4, 64, 128), BF16),
            pltpu.VMEM((2, 576, 256), F32),
            pltpu.VMEM((4, 2, 576, 128), BF16),
            pltpu.VMEM((4, 2, 576, 128), BF16),
            pltpu.SemaphoreType.DMA((200,)),
            pltpu.SemaphoreType.DMA((200,)),
            pltpu.SemaphoreType.DMA((16,)),
        ],
        compiler_params=pltpu.CompilerParams(
            collective_id=0, has_side_effects=True, vmem_limit_bytes=56 * 1024 * 1024
        ),
    )(
        jnp.swapaxes(tokens, 1, 2), gain.reshape(144, 128), w_query, w_keyval.T, w_out.T, cache, lengths
    )
    return jnp.swapaxes(out, 1, 2)


def solution(mesh):
    return jax.shard_map(
        body,
        mesh=mesh,
        in_specs=(
            P("gx", None, "yz"),
            P(),
            P("gx", "yz"),
            P("gx", "yz"),
            P("gx", "yz"),
            P("gx", "yz", None),
            P("gx"),
        ),
        out_specs=P("gx", None, "yz"),
        check_vma=False,
    )
```

```python
import math

import jax
import jax.numpy as jnp
from jax import lax
from jax.experimental import pallas as pl
from jax.experimental.pallas import tpu as pltpu
from jax.sharding import PartitionSpec as P

MESH = pl.DeviceIdType.MESH
HEAD = 256
F32 = jnp.float32
BF16 = jnp.bfloat16
LEFT = (((0,), (0,)), ((), ()))


class Wires:
    def __init__(self, send, recv):
        self.send, self.recv, self.used, self.all = send, recv, 0, []

    def __call__(self, src, dst, target):
        k = self.used
        self.used += 1
        copy = pltpu.make_async_remote_copy(
            src_ref=src, dst_ref=dst, send_sem=self.send.at[k], recv_sem=self.recv.at[k],
            device_id=target, device_id_type=MESH,
        )
        copy.start()
        self.all.append(copy)
        return copy


def near(v, d):
    return lax.rem(v + d + 4, 4)


def gather_plane(wires, unit, peer_y, peer_z, y, z, on_a=lambda j: None, on_b=lambda j: None, direct=False):
    yj = [y, near(y, -1), near(y, 1), near(y, 2)]
    zj = [z, near(z, -1), near(z, 1), near(z, 2)]

    def send(ref, target):
        return wires(ref, ref, target)

    zp, zm, yp, ym = [None] * 4, [None] * 4, [None] * 4, [None] * 4
    zfp, zfm, yfp, yfm = [None] * 4, [None] * 4, [None] * 4, [None] * 4

    def spread_a(j):
        zp[j] = send(unit(z, yj[j], 0, 2), peer_z(1))
        zm[j] = send(unit(z, yj[j], 0, 2), peer_z(-1))

    def spread_b(j):
        yp[j] = send(unit(zj[j], y, 2, 2), peer_y(1))
        ym[j] = send(unit(zj[j], y, 2, 2), peer_y(-1))

    def pass_a(j):
        zp[j].wait_recv()
        zfp[j] = send(unit(zj[1], yj[j], 0, 1), peer_z(1))
        zm[j].wait_recv()
        zfm[j] = send(unit(zj[2], yj[j], 1, 1), peer_z(-1))

    def pass_b(j):
        yp[j].wait_recv()
        yfp[j] = send(unit(zj[j], yj[1], 2, 1), peer_y(1))
        ym[j].wait_recv()
        yfm[j] = send(unit(zj[j], yj[2], 3, 1), peer_y(-1))

    a1p = send(unit(z, y, 0, 2), peer_y(1))
    b1p = send(unit(z, y, 2, 2), peer_z(1))
    a1m = send(unit(z, y, 0, 2), peer_y(-1))
    b1m = send(unit(z, y, 2, 2), peer_z(-1))
    spread_a(0)
    spread_b(0)
    if direct:
        a2p = send(unit(z, y, 0, 2), peer_y(2))
        b2p = send(unit(z, y, 2, 2), peer_z(2))
    yield
    a1p.wait_recv()
    if not direct:
        a2p = send(unit(z, yj[1], 0, 1), peer_y(1))
    spread_a(1)
    b1p.wait_recv()
    if not direct:
        b2p = send(unit(zj[1], y, 2, 1), peer_z(1))
    spread_b(1)
    yield
    a1m.wait_recv()
    a2 = [a2p]
    if not direct:
        a2.append(send(unit(z, yj[2], 1, 1), peer_y(-1)))
    spread_a(2)
    b1m.wait_recv()
    b2 = [b2p]
    if not direct:
        b2.append(send(unit(zj[2], y, 3, 1), peer_z(-1)))
    spread_b(2)
    yield
    pass_a(0)
    pass_b(0)
    yield
    for copy in a2:
        copy.wait_recv()
    spread_a(3)
    for copy in b2:
        copy.wait_recv()
    spread_b(3)
    yield
    on_b(0)
    for j in range(1, 4):
        pass_a(j)
        pass_b(j)
        zfp[j - 1].wait_recv()
        zfm[j - 1].wait_recv()
        on_a(j - 1)
        yield
    on_b(1)
    on_b(2)
    for copy in (zfp[3], zfm[3]):
        copy.wait_recv()
    on_a(3)
    for j in range(4):
        yfp[j].wait_recv()
        yfm[j].wait_recv()
    on_b(3)


def gather_direct(wires, unit, peer_y, peer_z, y, z, on_a=lambda j: None, on_b=lambda j: None):
    yj = [y, near(y, -1), near(y, 1), near(y, 2)]
    zj = [z, near(z, -1), near(z, 1), near(z, 2)]
    ways = (1, -1, 2)

    def send(ref, peer):
        return [wires(ref, ref, peer(d)) for d in ways]

    own_a, own_b = unit(z, y, 0, 2), unit(z, y, 2, 2)
    a1, b1 = send(own_a, peer_y), send(own_b, peer_z)
    a2, b2 = [send(own_a, peer_z)], [send(own_b, peer_y)]
    yield
    for j in range(3):
        a1[j].wait_recv()
        a2.append(send(unit(z, yj[j + 1], 0, 2), peer_z))
        b1[j].wait_recv()
        b2.append(send(unit(zj[j + 1], y, 2, 2), peer_y))
        yield
    on_b(0)
    for j in range(4):
        for copy in a2[j]:
            copy.wait_recv()
        on_a(j)
        yield
    for j in (1, 2, 3):
        for k in range(4):
            b2[k][j - 1].wait_recv()
        on_b(j)


def gather_lines(wires, unit, peer_y, peer_z, y, z):
    yj = [y, near(y, -1), near(y, 1), near(y, 2)]
    zj = [z, near(z, -1), near(z, 1), near(z, 2)]

    def send(ref, target):
        return wires(ref, ref, target)

    def spread(j):
        ref = unit(zj[j], y, None)
        return [send(ref, peer_y(1)), send(ref, peer_y(-1))]

    def hand_on(j, pair):
        pair[0].wait_recv()
        first = send(unit(zj[j], yj[1], 0), peer_y(1))
        pair[1].wait_recv()
        return [first, send(unit(zj[j], yj[2], 1), peer_y(-1))]

    own = unit(z, y, None)
    along = [send(own, peer_z(d)) for d in (1, -1, 2)]
    near_y = [spread(0)]
    yield
    for j in (1, 2):
        along[j - 1].wait_recv()
        near_y.append(spread(j))
    far_y = [hand_on(0, near_y[0])]
    yield
    along[2].wait_recv()
    near_y.append(spread(3))
    for j in (1, 2, 3):
        yield
        far_y.append(hand_on(j, near_y[j]))
    yield
    for pair in far_y:
        for copy in pair:
            copy.wait_recv()


def kernel(
    tokens, gain, w_query, w_keyval, w_out, cache, lengths, out,
    mine, raw, stat_y, stat_z, stat_x, gain_col, whole, w_rows, w_t, wo, acc, q_send, q_recv, kv_send, kv_recv,
    kv_t, slots, values_t, cosine, sine, scores, weights, queries, heads, heads_all, acc_o, o_send, o_recv,
    send_sem, recv_sem, local_sem, block_send, block_recv, swap_sem,
):
    x = lax.axis_index("gx")
    yz = lax.axis_index("yz")
    z, y, c = yz // 8, (yz // 2) % 4, yz % 2

    def device(xx, zz, yy, cc):
        return (xx, zz * 8 + yy * 2 + cc)

    peer_x = lambda d, dc=0: device(near(x, d), z, y, lax.rem(c + dc, 2))
    peer_y = lambda d: device(x, z, near(y, d), c)
    peer_z = lambda d, dc=0: device(x, near(z, d), y, lax.rem(c + dc, 2))
    sibling = device(x, z, y, 1 - c)

    barrier = pltpu.get_barrier_semaphore()
    peers = [sibling]
    for d in (1, 2, 3):
        peers += [peer_x(d), peer_x(d, 1), peer_z(d), peer_z(d, 1), peer_y(d)]
    twin = device(3 - x, 3 - z, y, c)
    peers.append(twin)
    for p in peers:
        pl.semaphore_signal(barrier, inc=1, device_id=p, device_id_type=MESH)

    locals_ = []

    def local(src, dst):
        copy = pltpu.make_async_copy(src, dst, local_sem.at[len(locals_)])
        copy.start()
        locals_.append(copy)
        return copy

    quarter = lambda k: pl.ds(pl.multiple_of(k * 144, 16), 144)
    own_mine = local(tokens.at[0], mine)
    slot_rows = pl.ds(pl.multiple_of(yz * 64, 64), 64)
    own_slots = local(cache.at[0], slots.at[slot_rows, :])
    own_raw = local(tokens.at[0, quarter(z), :], raw.at[z])
    own_rows = local(w_query, w_rows)
    kv_rows16 = pl.ds(pl.multiple_of(512 + c * 16, 16), 16)
    own_kv = local(w_keyval, w_t.at[kv_rows16, :])
    pair = x // 2
    partner = device(x + 1 - 2 * (x % 2), z, y, c)
    wo_lanes = pl.ds(pl.multiple_of((x % 2) * 2048, 128), 2048)
    wo_other = pl.ds(pl.multiple_of((1 - x % 2) * 2048, 128), 2048)
    own_wo = local(w_out, wo.at[c, :, wo_lanes])
    wo_rows = lambda k: pl.ds(k * 48, 48)

    def lend(k):
        return wires(w_out.at[wo_rows(k), :], wo.at[c, wo_rows(k), wo_lanes], partner)


    pl.semaphore_wait(barrier, len(peers))
    wires = Wires(send_sem, recv_sem)
    first = [wires(tokens.at[0, quarter(near(z, d)), :], raw.at[z], peer_z(d)) for d in (1, 3, 2)]

    spot = whole.at[x // 2, y, x % 2, c, z]
    half_lanes = lambda k: pl.ds(pl.multiple_of(k * 128, 128), 128)

    def block(e, dc):
        i, cc = near(z, e), lax.rem(c + dc, 2)
        return pltpu.make_async_remote_copy(
            src_ref=raw.at[i, :, half_lanes(cc)], dst_ref=spot, send_sem=block_send.at[e * 2 + dc],
            recv_sem=block_recv.at[x * 2 + c], device_id=device(i, z, y, cc), device_id_type=MESH,
        )

    def start_block(e):
        @pl.when(near(z, e) == x)
        def _():
            pltpu.make_async_copy(raw.at[x, :, half_lanes(c)], spot, block_recv.at[x * 2 + c]).start()

        @pl.when(near(z, e) != x)
        def _():
            block(e, 0).start()

        block(e, 1).start()

    own_raw.wait()
    start_block(0)
    lent = [lend(k) for k in range(0)]

    own_mine.wait()
    v = mine[...].astype(F32)
    mean = jnp.sum(v, axis=0, keepdims=True) * (1.0 / 576)
    square = jnp.sum((v - mean) * (v - mean), axis=0, keepdims=True)
    row = lax.broadcasted_iota(jnp.int32, (8, 256), 0)

    def join(ref, count, size):
        means = [ref[k][0:1] for k in range(count)]
        mid = sum(means[1:], means[0]) * (1.0 / count)
        total = sum([ref[k][1:2] for k in range(1, count)], ref[0][1:2])
        for m in means:
            total = total + size * (m - mid) * (m - mid)
        return mid, total

    stat_y[y] = jnp.where(row == 0, mean, square)
    stat_1 = [wires(stat_y.at[y], stat_y.at[y], peer_y(d)) for d in (1, 3, 2)]
    own_slots.wait()

    def cache_unit(zz, yy, part):
        at = (zz * 8 + yy * 2 + c) * 64 + (0 if part is None else part * 32)
        return slots.at[pl.ds(pl.multiple_of(at, 32), 64 if part is None else 32), :]

    cached = gather_lines(wires, cache_unit, peer_y, peer_z, y, z)
    next(cached)

    lane = lax.broadcasted_iota(jnp.int32, (16, 128), 1)
    sub = lax.broadcasted_iota(jnp.int32, (16, 128), 0)

    for k in range(18):
        g = x * 288 + y * 72 + (k // 9) * 36 + z * 9 + k % 9
        line = jnp.broadcast_to(gain[pl.ds(g // 8, 1), :], (16, 128))
        col = jnp.sum(jnp.where(lane == sub + (g % 8) * 16, line, 0.0), axis=1, keepdims=True)
        gain_col[k * 16:(k + 1) * 16, :] = jnp.broadcast_to(col, (16, 128))

    for copy in stat_1:
        copy.wait_recv()
    mean, square = join(stat_y, 4, 576.0)
    me = z * 2 + c
    stat_z[me] = jnp.where(row == 0, mean, square)
    stat_2 = []
    for d in (1, 3, 2):
        for dc in (0, 1):
            stat_2.append(wires(stat_z.at[me], stat_z.at[me], peer_z(d, dc)))
    stat_2.append(wires(stat_z.at[me], stat_z.at[me], sibling))
    first[0].wait_recv()
    start_block(3)
    first[1].wait_recv()
    start_block(1)
    next(cached)
    for copy in stat_2:
        copy.wait_recv()
    mean, square = join(stat_z, 8, 2304.0)
    stat_x[x] = jnp.where(row == 0, mean, lax.rsqrt(square * (1.0 / 18432) + 1e-6))
    stat_3 = [wires(stat_x.at[x], stat_x.at[x], peer_x(d)) for d in (1, 3, 2)]
    first[2].wait_recv()
    start_block(2)
    next(cached)
    next(cached)
    for k in range(8):
        pltpu.make_async_copy(raw.at[0, :, 0:128], whole.at[k // 4, y, (k // 2) % 2, k % 2, z], block_recv.at[k]).wait()
    for copy in stat_3:
        copy.wait_recv()
    for b in range(4):
        norm = stat_x[b, :, half_lanes(c)]
        for k in range(2):
            v = whole[b // 2, y, b % 2, k, z].astype(F32)
            v = (v - norm[0:1]) * norm[1:2] * gain_col[k * 144:(k + 1) * 144, :]
            whole[b // 2, y, b % 2, k, z] = v.astype(BF16)
    for e in range(4):
        @pl.when(near(z, e) != x)
        def _():
            block(e, 0).wait_send()

        block(e, 1).wait_send()


    def unit(zz, yy, start, count):
        if count == 2:
            return whole.at[start // 2, yy, :, :, zz]
        return whole.at[start // 2, yy, start % 2, :, zz]

    def project(half, yy, fresh_start):
        right = jnp.concatenate([whole[half, yy, b].reshape(1152, 128) for b in range(2)], axis=1)
        left = w_t[:, pl.ds(pl.multiple_of(yy * 1152, 128), 1152)]
        part = jnp.dot(left, right, preferred_element_type=F32)
        if fresh_start:
            acc[half] = part
        else:
            acc[half] += part

    yj = [y, near(y, -1), near(y, 1), near(y, 2)]
    lent += [lend(k) for k in range(0, 7)]
    gathered = gather_plane(wires, unit, peer_y, peer_z, y, z, lambda j: project(0, yj[j], j == 0), lambda j: project(1, yj[j], j == 0))
    next(gathered)
    next(gathered)
    next(gathered)
    own_rows.wait()
    w_mine = pl.ds(pl.multiple_of(c * 256, 256), 256)

    @pl.loop(0, 18)
    def _(s):
        at = pl.ds(pl.multiple_of(s * 256, 256), 256)
        w_t[w_mine, at] = w_rows[at, :].T

    own_kv.wait()
    own_wo.wait()
    shared = [
        wires(w_t.at[w_mine, :], w_t.at[w_mine, :], sibling),
        wires(w_keyval, w_t.at[kv_rows16, :], sibling),
        wires(w_out, wo.at[c, :, wo_lanes], sibling),
    ]
    next(gathered)
    next(cached)
    next(cached)
    for copy in shared[:2]:
        copy.wait_recv()
    next(gathered)
    for _ in cached:
        pass
    share = slots.reshape(16, 2, 64, 512).at[:, c]
    share_slots = wires(share, share, sibling)
    freq = jnp.exp(
        lax.broadcasted_iota(jnp.int32, (128, 256), 0).astype(F32) * (-2.0 * math.log(10000.0) / HEAD)
    )
    angle = (lengths[0] + lax.broadcasted_iota(jnp.int32, (128, 256), 1)).astype(F32) * freq
    cosine[...] = jnp.cos(angle)
    sine[...] = jnp.sin(angle)
    for _ in gathered:
        pass
    for b in range(4):
        lanes = slice((b % 2) * 128, (b % 2) * 128 + 128)
        kv_send[b] = acc[b // 2, 512:544, lanes]
        q_send[b] = acc[b // 2, 0:512, lanes].astype(BF16)
    third, fourth = [], []
    for d in (1, 3, 2):
        third.append(wires(kv_send.at[near(x, d)], kv_recv.at[x], peer_x(d)))
    for d in (1, 3, 2):
        fourth.append(wires(q_send.at[near(x, d)], q_recv.at[x], peer_x(d)))
    for copy in third:
        copy.wait_recv()
    total = kv_send[x]
    for d in (1, 2, 3):
        total = total + kv_recv[near(x, d)]
    kv_block = lambda zz, yy: kv_t.at[c, pl.ds(pl.multiple_of((zz * 4 + yy) * 32, 32), 32), :]
    kv_t[c, pl.ds(pl.multiple_of((z * 4 + y) * 32, 32), 32), :] = total.astype(BF16)
    kv_y = [wires(kv_block(z, y), kv_block(z, y), peer_y(d)) for d in (1, 3, 2)]
    for copy in kv_y:
        copy.wait_recv()
    kv_rows = kv_t.at[c, pl.ds(pl.multiple_of(z * 128, 128), 128), :]
    kv_z = [wires(kv_rows, kv_rows, sibling)]
    for d in (1, 3, 2):
        for dc in (0, 1):
            kv_z.append(wires(kv_rows, kv_rows, peer_z(d, dc)))
    share_slots.wait_recv()

    @pl.loop(0, 8)
    def _(s):
        at = pl.ds(pl.multiple_of(s * 256, 256), 256)
        values_t[:, at] = slots[at, 256:512].T


    for copy in fourth:
        copy.wait_recv()
    lent += [lend(k) for k in range(7, 12)]
    query = q_send[x].astype(F32)
    for d in (1, 2, 3):
        query = query + q_recv[near(x, d)].astype(F32)
    cos_q, sin_q = cosine[:, half_lanes(c)], sine[:, half_lanes(c)]
    for h in range(2):
        u, w = query[h * 256:h * 256 + 128], query[h * 256 + 128:h * 256 + 256]
        queries[0:128, h * 128:(h + 1) * 128] = (u * cos_q - w * sin_q).astype(BF16)
        queries[128:256, h * 128:(h + 1) * 128] = (w * cos_q + u * sin_q).astype(BF16)
    inv = 1.0 / math.sqrt(HEAD)

    def fold(s, f):
        return f(s.reshape(s.shape[0] // 8, 8, 256), axis=0)

    def cached_scores(k, top):
        at = pl.ds(pl.multiple_of(k * 256, 256), 256)
        s = jnp.dot(slots[at, 0:256], queries[...], preferred_element_type=F32) * inv
        slot = k * 256 + lax.broadcasted_iota(jnp.int32, (256, 256), 0)
        s = jnp.where(slot < lengths[0], s, -1e30)
        scores[at, :] = s
        return jnp.maximum(top, fold(s, jnp.max))

    top = lax.fori_loop(0, 8, cached_scores, jnp.full((8, 256), -1e30, F32))
    for copy in kv_z:
        copy.wait_recv()
    kv = jnp.concatenate([kv_t[0], kv_t[1]], axis=1)
    u, w = kv[0:128].astype(F32), kv[128:256].astype(F32)
    fresh = jnp.concatenate([u * cosine[...] - w * sine[...], w * cosine[...] + u * sine[...]], axis=0).astype(BF16)
    s = lax.dot_general(fresh, queries[...], LEFT, preferred_element_type=F32) * inv
    t = c * 128 + lax.rem(lax.broadcasted_iota(jnp.int32, (256, 256), 1), 128)
    t2 = lax.broadcasted_iota(jnp.int32, (256, 256), 0)
    s = jnp.where(t2 <= t, s, -1e30)
    scores[2048:2304, :] = s
    top = jnp.max(jnp.maximum(top, fold(s, jnp.max)), axis=0, keepdims=True)

    def exponentials(k, total):
        at = pl.ds(pl.multiple_of(k * 256, 256), 256)
        p = jnp.exp(scores[at, :] - top)
        weights[at, :] = p.astype(BF16)
        return total + fold(p, jnp.sum)

    total = jnp.sum(lax.fori_loop(0, 9, exponentials, jnp.zeros((8, 256), F32)), axis=0, keepdims=True)
    summed = jnp.dot(values_t[...], weights[0:2048, :], preferred_element_type=F32)
    summed += jnp.dot(kv[256:512], weights[2048:2304, :], preferred_element_type=F32)
    done = (summed / total).astype(BF16)
    heads[0] = done[:, 0:128]
    heads[1] = done[:, 128:256]

    stays = z // 2 == pair
    swap = pltpu.make_async_remote_copy(
        src_ref=heads, dst_ref=heads_all.at[y, 3 - z], send_sem=swap_sem.at[0], recv_sem=swap_sem.at[1],
        device_id=twin, device_id_type=MESH,
    )
    keep = pltpu.make_async_copy(heads, heads_all.at[y, z], swap_sem.at[1])
    pl.when(stays)(keep.start)
    pl.when(jnp.logical_not(stays))(swap.start)
    passed = []
    for k in range(7):
        lent[k].wait_recv()
        passed.append(wires(wo.at[c, wo_rows(k), wo_other], wo.at[c, wo_rows(k), wo_other], sibling))
    shared[2].wait_recv()
    keep.wait()
    pl.when(jnp.logical_not(stays))(swap.wait_send)

    def head_unit(zz, yy, start, count):
        return heads_all.at[yy, zz, start // 2, (start % 2) * 128:(start % 2 + count) * 128, :]

    def project_out(h, yy, fresh_start):
        rights, lanes = [], []
        for j in range(2):
            block = 2 * pair + j
            rights.append(jnp.concatenate([heads_all[yy, block, h], heads_all[yy, 3 - block, h]], axis=1))
            lanes.append(pl.ds(pl.multiple_of(j * 2048 + yy * 512 + h * 256, 128), 256))
        right = jnp.concatenate(rights, axis=0)
        for k in range(2):
            left = jnp.concatenate([wo[k, :, lanes[0]], wo[k, :, lanes[1]]], axis=1)
            part = jnp.dot(left, right, preferred_element_type=F32)
            if fresh_start:
                acc_o[k] = part
            else:
                acc_o[k] += part

    begun = []

    def absorb(h, j):
        if not begun:
            for copy in passed:
                copy.wait_recv()
        project_out(h, yj[j], not begun)
        begun.append(j)

    heads_gather = gather_plane(wires, head_unit, peer_y, peer_z, y, z, lambda j: absorb(0, j), lambda j: absorb(1, j), direct=True)
    for step in range(4):
        next(heads_gather)
    for k in range(7, 12):
        lent[k].wait_recv()
        passed.append(wires(wo.at[c, wo_rows(k), wo_other], wo.at[c, wo_rows(k), wo_other], sibling))
    for _ in heads_gather:
        pass
    for k in range(2):
        o_send[0, k] = acc_o[k, :, 128:256].astype(BF16)
    last = [
        wires(o_send.at[0, lax.rem(c + dc, 2)], o_recv.at[0, c], device(3 - x, z, y, lax.rem(c + dc, 2))) for dc in (0, 1)
    ]
    o_send[1, 1 - c] = acc_o[1 - c, :, 0:128].astype(BF16)
    last.append(wires(o_send.at[1, 1 - c], o_recv.at[1, c], sibling))
    for copy in last:
        copy.wait_recv()
    out[0, :, half_lanes(c)] = (acc_o[c, :, 0:128] + o_recv[0, c].astype(F32)).astype(BF16)
    other = o_recv[1, 1 - c].astype(F32) + o_recv[0, 1 - c].astype(F32)
    out[0, :, half_lanes(1 - c)] = other.astype(BF16)

    for copy in wires.all:
        copy.wait_send()


def body(tokens, gain, w_query, w_keyval, w_out, cache, lengths):
    hbm = pl.BlockSpec(memory_space=pl.ANY)
    vmem = pl.BlockSpec(memory_space=pltpu.VMEM)
    smem = pl.BlockSpec(memory_space=pltpu.SMEM)
    out = pl.pallas_call(
        kernel,
        out_shape=jax.ShapeDtypeStruct((1, 576, 256), BF16),
        in_specs=[hbm, vmem, hbm, hbm, hbm, hbm, smem],
        out_specs=vmem,
        scratch_shapes=[
            pltpu.VMEM((576, 256), BF16),
            pltpu.VMEM((4, 144, 256), BF16),
            pltpu.VMEM((4, 8, 256), F32),
            pltpu.VMEM((8, 8, 256), F32),
            pltpu.VMEM((4, 8, 256), F32),
            pltpu.VMEM((288, 128), F32),
            pltpu.VMEM((2, 4, 2, 2, 4, 144, 128), BF16),
            pltpu.VMEM((4608, 256), BF16),
            pltpu.VMEM((544, 4608), BF16),
            pltpu.VMEM((2, 576, 4096), BF16),
            pltpu.VMEM((2, 544, 256), F32),
            pltpu.VMEM((4, 512, 128), BF16),
            pltpu.VMEM((4, 512, 128), BF16),
            pltpu.VMEM((4, 32, 128), F32),
            pltpu.VMEM((4, 32, 128), F32),
            pltpu.VMEM((2, 512, 128), BF16),
            pltpu.VMEM((2048, 512), BF16),
            pltpu.VMEM((256, 2048), BF16),
            pltpu.VMEM((128, 256), F32),
            pltpu.VMEM((128, 256), F32),
            pltpu.VMEM((2304, 256), F32),
            pltpu.VMEM((2304, 256), BF16),
            pltpu.VMEM((256, 256), BF16),
            pltpu.VMEM((2, 256, 128), BF16),
            pltpu.VMEM((4, 4, 2, 256, 128), BF16),
            pltpu.VMEM((2, 576, 256), F32),
            pltpu.VMEM((2, 2, 576, 128), BF16),
            pltpu.VMEM((2, 2, 576, 128), BF16),
            pltpu.SemaphoreType.DMA((240,)),
            pltpu.SemaphoreType.DMA((240,)),
            pltpu.SemaphoreType.DMA((16,)),
            pltpu.SemaphoreType.DMA((8,)),
            pltpu.SemaphoreType.DMA((8,)),
            pltpu.SemaphoreType.DMA((2,)),
        ],
        compiler_params=pltpu.CompilerParams(
            collective_id=0, has_side_effects=True, vmem_limit_bytes=56 * 1024 * 1024
        ),
    )(
        jnp.swapaxes(tokens, 1, 2), gain.reshape(144, 128), w_query, w_keyval.T, w_out.T, cache, lengths
    )
    return jnp.swapaxes(out, 1, 2)


def solution(mesh):
    return jax.shard_map(
        body,
        mesh=mesh,
        in_specs=(
            P("gx", None, "yz"),
            P(),
            P("gx", "yz"),
            P("gx", "yz"),
            P("gx", "yz"),
            P("gx", "yz", None),
            P("gx"),
        ),
        out_specs=P("gx", None, "yz"),
        check_vma=False,
    )
```

```python
import math

import jax
import jax.numpy as jnp
from jax import lax
from jax.experimental import pallas as pl
from jax.experimental.pallas import tpu as pltpu
from jax.sharding import PartitionSpec as P

MESH = pl.DeviceIdType.MESH
HEAD = 256
F32 = jnp.float32
BF16 = jnp.bfloat16
LEFT = (((0,), (0,)), ((), ()))
POOL = 72
RECV = 77


class Wires:
    def __init__(self, send, recv, pool):
        self.send, self.recv, self.pool, self.used, self.all = send, recv, pool, 0, []

    def __call__(self, src, dst, target):
        self.used += 1
        return self.start(src, dst, target, self.recv.at[self.used - 1])

    def branch(self, recv):
        slots = iter(range(64))
        return lambda src, dst, target: self.start(src, dst, target, recv.at[next(slots)])

    def start(self, src, dst, target, recv):
        n = len(self.all)
        if n >= self.pool:
            self.all[n - self.pool].wait_send()
        copy = pltpu.make_async_remote_copy(
            src_ref=src, dst_ref=dst, send_sem=self.send.at[n % self.pool], recv_sem=recv,
            device_id=target, device_id_type=MESH,
        )
        copy.start()
        self.all.append(copy)
        return copy

    def finish(self):
        for copy in self.all[-self.pool:]:
            copy.wait_send()


def near(v, d):
    return lax.rem(v + d + 4, 4)


def gather_plane(wires, unit, peer_y, peer_z, y, z, on_a=lambda j: None, on_b=lambda j: None, direct=False):
    yj = [y, near(y, -1), near(y, 1), near(y, 2)]
    zj = [z, near(z, -1), near(z, 1), near(z, 2)]

    def send(ref, target):
        return wires(ref, ref, target)

    zp, zm, yp, ym = [None] * 4, [None] * 4, [None] * 4, [None] * 4
    zfp, zfm, yfp, yfm = [None] * 4, [None] * 4, [None] * 4, [None] * 4

    def spread_a(j):
        zp[j] = send(unit(z, yj[j], 0, 2), peer_z(1))
        zm[j] = send(unit(z, yj[j], 0, 2), peer_z(-1))

    def spread_b(j):
        yp[j] = send(unit(zj[j], y, 2, 2), peer_y(1))
        ym[j] = send(unit(zj[j], y, 2, 2), peer_y(-1))

    def pass_a(j):
        zp[j].wait_recv()
        zfp[j] = send(unit(zj[1], yj[j], 0, 1), peer_z(1))
        zm[j].wait_recv()
        zfm[j] = send(unit(zj[2], yj[j], 1, 1), peer_z(-1))

    def pass_b(j):
        yp[j].wait_recv()
        yfp[j] = send(unit(zj[j], yj[1], 2, 1), peer_y(1))
        ym[j].wait_recv()
        yfm[j] = send(unit(zj[j], yj[2], 3, 1), peer_y(-1))

    a1p = send(unit(z, y, 0, 2), peer_y(1))
    b1p = send(unit(z, y, 2, 2), peer_z(1))
    a1m = send(unit(z, y, 0, 2), peer_y(-1))
    b1m = send(unit(z, y, 2, 2), peer_z(-1))
    spread_a(0)
    spread_b(0)
    if direct:
        a2p = send(unit(z, y, 0, 2), peer_y(2))
        b2p = send(unit(z, y, 2, 2), peer_z(2))
    yield
    a1p.wait_recv()
    if not direct:
        a2p = send(unit(z, yj[1], 0, 1), peer_y(1))
    spread_a(1)
    b1p.wait_recv()
    if not direct:
        b2p = send(unit(zj[1], y, 2, 1), peer_z(1))
    spread_b(1)
    yield
    a1m.wait_recv()
    a2 = [a2p]
    if not direct:
        a2.append(send(unit(z, yj[2], 1, 1), peer_y(-1)))
    spread_a(2)
    b1m.wait_recv()
    b2 = [b2p]
    if not direct:
        b2.append(send(unit(zj[2], y, 3, 1), peer_z(-1)))
    spread_b(2)
    yield
    pass_a(0)
    pass_b(0)
    yield
    for copy in a2:
        copy.wait_recv()
    spread_a(3)
    for copy in b2:
        copy.wait_recv()
    spread_b(3)
    yield
    for j in range(1, 4):
        pass_a(j)
        pass_b(j)
        if j == 2:
            on_b(0)
            zfp[0].wait_recv()
            zfm[0].wait_recv()
            on_a(0)
        yield
    for j in (1, 2):
        zfp[j].wait_recv()
        zfm[j].wait_recv()
        on_a(j)
    on_b(1)
    on_b(2)
    for copy in (zfp[3], zfm[3]):
        copy.wait_recv()
    on_a(3)
    for j in range(4):
        yfp[j].wait_recv()
        yfm[j].wait_recv()
    on_b(3)


def gather_direct(wires, unit, peer_y, peer_z, y, z, on_a=lambda j: None, on_b=lambda j: None):
    yj = [y, near(y, -1), near(y, 1), near(y, 2)]
    zj = [z, near(z, -1), near(z, 1), near(z, 2)]
    ways = (1, -1, 2)

    def send(ref, peer):
        return [wires(ref, ref, peer(d)) for d in ways]

    own_a, own_b = unit(z, y, 0, 2), unit(z, y, 2, 2)
    a1, b1 = send(own_a, peer_y), send(own_b, peer_z)
    a2, b2 = [send(own_a, peer_z)], [send(own_b, peer_y)]
    yield
    for j in range(3):
        a1[j].wait_recv()
        a2.append(send(unit(z, yj[j + 1], 0, 2), peer_z))
        b1[j].wait_recv()
        b2.append(send(unit(zj[j + 1], y, 2, 2), peer_y))
        yield
    on_b(0)
    for j in range(4):
        for copy in a2[j]:
            copy.wait_recv()
        on_a(j)
        yield
    for j in (1, 2, 3):
        for k in range(4):
            b2[k][j - 1].wait_recv()
        on_b(j)


def gather_lines(wires, unit, peer_y, peer_z, y, z):
    yj = [y, near(y, -1), near(y, 1), near(y, 2)]
    zj = [z, near(z, -1), near(z, 1), near(z, 2)]

    def send(ref, target):
        return wires(ref, ref, target)

    def spread(j):
        ref = unit(zj[j], y, None)
        return [send(ref, peer_y(1)), send(ref, peer_y(-1))]

    def hand_on(j, pair):
        pair[0].wait_recv()
        first = send(unit(zj[j], yj[1], 0), peer_y(1))
        pair[1].wait_recv()
        return [first, send(unit(zj[j], yj[2], 1), peer_y(-1))]

    own = unit(z, y, None)
    along = [send(own, peer_z(d)) for d in (1, -1, 2)]
    near_y = [spread(0)]
    yield
    for j in (1, 2):
        along[j - 1].wait_recv()
        near_y.append(spread(j))
    far_y = [hand_on(0, near_y[0])]
    yield
    along[2].wait_recv()
    near_y.append(spread(3))
    for j in (1, 2, 3):
        yield
        far_y.append(hand_on(j, near_y[j]))
    yield
    for pair in far_y:
        for copy in pair:
            copy.wait_recv()


def kernel(
    tokens, gain, w_query, w_keyval, w_out, cache, lengths, out,
    mine, raw, stat_y, stat_z, stat_x, gain_col, whole, w_rows, w_t, wo, acc, q_send, q_recv, kv_send, kv_recv,
    kv_t, slots, values_t, cosine, sine, scores, weights, queries, heads, heads_all, acc_o, o_send, o_recv,
    send_sem, recv_sem, gather_sem, local_sem, block_send, block_recv, swap_send, swap_recv,
):
    x = lax.axis_index("gx")
    yz = lax.axis_index("yz")
    z, y, c = yz // 8, (yz // 2) % 4, yz % 2

    def device(xx, zz, yy, cc):
        return (xx, zz * 8 + yy * 2 + cc)

    peer_x = lambda d, dc=0: device(near(x, d), z, y, lax.rem(c + dc, 2))
    peer_y = lambda d, dc=0: device(x, z, near(y, d), lax.rem(c + dc, 2))
    peer_z = lambda d, dc=0: device(x, near(z, d), y, lax.rem(c + dc, 2))
    sibling = device(x, z, y, 1 - c)

    barrier = pltpu.get_barrier_semaphore()
    peers = [sibling]
    for d in (1, 2, 3):
        peers += [peer_x(d), peer_x(d, 1), peer_z(d), peer_z(d, 1), peer_y(d), peer_y(d, 1)]
    twin = device(3 - x, 3 - z, y, c)
    peers.append(twin)
    for p in peers:
        pl.semaphore_signal(barrier, inc=1, device_id=p, device_id_type=MESH)

    locals_ = []

    def local(src, dst):
        copy = pltpu.make_async_copy(src, dst, local_sem.at[len(locals_)])
        copy.start()
        locals_.append(copy)
        return copy

    quarter = lambda k: pl.ds(pl.multiple_of(k * 144, 16), 144)
    own_mine = local(tokens.at[0], mine)
    slot_rows = pl.ds(pl.multiple_of(yz * 64, 64), 64)
    own_slots = local(cache.at[0], slots.at[slot_rows, :])
    own_raw = local(tokens.at[0, quarter(z), :], raw.at[z])
    own_rows = local(w_query, w_rows)
    kv_rows16 = pl.ds(pl.multiple_of(512 + c * 16, 16), 16)
    own_kv = local(w_keyval, w_t.at[kv_rows16, :])
    pair = x // 2
    partner = device(x + 1 - 2 * (x % 2), z, y, c)
    wo_lanes = pl.ds(pl.multiple_of((x % 2) * 2048, 128), 2048)
    wo_other = pl.ds(pl.multiple_of((1 - x % 2) * 2048, 128), 2048)
    own_wo = local(w_out, wo.at[c, :, wo_lanes])
    wo_rows = lambda k: pl.ds((0, 96, 432)[k], (96, 336, 144)[k])

    def lend(k):
        return wires(w_out.at[wo_rows(k), :], wo.at[c, wo_rows(k), wo_lanes], partner)


    pl.semaphore_wait(barrier, len(peers))
    wires = Wires(send_sem, recv_sem, POOL)
    first = [wires(tokens.at[0, quarter(near(z, d)), :], raw.at[z], peer_z(d)) for d in (1, 3, 2)]

    spot = whole.at[x // 2, y, x % 2, c, z]
    half_lanes = lambda k: pl.ds(pl.multiple_of(k * 128, 128), 128)

    def block(e, dc):
        i, cc = near(z, e), lax.rem(c + dc, 2)
        return pltpu.make_async_remote_copy(
            src_ref=raw.at[i, :, half_lanes(cc)], dst_ref=spot, send_sem=block_send.at[e * 2 + dc],
            recv_sem=block_recv.at[x * 2 + c], device_id=device(i, z, y, cc), device_id_type=MESH,
        )

    def start_block(e):
        @pl.when(near(z, e) == x)
        def _():
            pltpu.make_async_copy(raw.at[x, :, half_lanes(c)], spot, block_recv.at[x * 2 + c]).start()

        @pl.when(near(z, e) != x)
        def _():
            block(e, 0).start()

        block(e, 1).start()

    own_raw.wait()
    start_block(0)
    lent = [lend(0)]

    own_mine.wait()
    v = mine[...].astype(F32)
    mean = jnp.sum(v, axis=0, keepdims=True) * (1.0 / 576)
    square = jnp.sum((v - mean) * (v - mean), axis=0, keepdims=True)
    row = lax.broadcasted_iota(jnp.int32, (8, 256), 0)

    def join(ref, count, size):
        means = [ref[k][0:1] for k in range(count)]
        mid = sum(means[1:], means[0]) * (1.0 / count)
        total = sum([ref[k][1:2] for k in range(1, count)], ref[0][1:2])
        for m in means:
            total = total + size * (m - mid) * (m - mid)
        return mid, total

    stat_y[y] = jnp.where(row == 0, mean, square)
    stat_1 = [wires(stat_y.at[y], stat_y.at[y], peer_y(d)) for d in (1, 3, 2)]
    own_slots.wait()

    def cache_unit(zz, yy, part):
        at = (zz * 8 + yy * 2 + c) * 64 + (0 if part is None else part * 32)
        return slots.at[pl.ds(pl.multiple_of(at, 32), 64 if part is None else 32), :]

    cached = gather_lines(wires, cache_unit, peer_y, peer_z, y, z)
    next(cached)

    lane = lax.broadcasted_iota(jnp.int32, (16, 128), 1)
    sub = lax.broadcasted_iota(jnp.int32, (16, 128), 0)

    for k in range(18):
        g = x * 288 + y * 72 + (k // 9) * 36 + z * 9 + k % 9
        line = jnp.broadcast_to(gain[pl.ds(g // 8, 1), :], (16, 128))
        col = jnp.sum(jnp.where(lane == sub + (g % 8) * 16, line, 0.0), axis=1, keepdims=True)
        gain_col[k * 16:(k + 1) * 16, :] = jnp.broadcast_to(col, (16, 128))

    freq = jnp.exp(
        lax.broadcasted_iota(jnp.int32, (128, 256), 0).astype(F32) * (-2.0 * math.log(10000.0) / HEAD)
    )
    angle = (lengths[0] + lax.broadcasted_iota(jnp.int32, (128, 256), 1)).astype(F32) * freq
    cosine[...] = jnp.cos(angle)
    sine[...] = jnp.sin(angle)
    for copy in stat_1:
        copy.wait_recv()
    mean, square = join(stat_y, 4, 576.0)
    me = z * 2 + c
    stat_z[me] = jnp.where(row == 0, mean, square)
    stat_2 = []
    for d in (1, 3, 2):
        for dc in (0, 1):
            stat_2.append(wires(stat_z.at[me], stat_z.at[me], peer_z(d, dc)))
    stat_2.append(wires(stat_z.at[me], stat_z.at[me], sibling))
    first[0].wait_recv()
    start_block(3)
    first[1].wait_recv()
    start_block(1)
    next(cached)
    for copy in stat_2:
        copy.wait_recv()
    mean, square = join(stat_z, 8, 2304.0)
    stat_x[x] = jnp.where(row == 0, mean, lax.rsqrt(square * (1.0 / 18432) + 1e-6))
    stat_3 = [wires(stat_x.at[x], stat_x.at[x], peer_x(d)) for d in (1, 3, 2)]
    first[2].wait_recv()
    start_block(2)
    next(cached)
    next(cached)
    own_rows.wait()
    w_mine = pl.ds(pl.multiple_of(c * 256, 256), 256)

    @pl.loop(0, 18)
    def _(s):
        at = pl.ds(pl.multiple_of(s * 256, 256), 256)
        w_t[w_mine, at] = w_rows[at, :].T

    for k in range(8):
        pltpu.make_async_copy(raw.at[0, :, 0:128], whole.at[k // 4, y, (k // 2) % 2, k % 2, z], block_recv.at[k]).wait()
    for copy in stat_3:
        copy.wait_recv()
    for b in range(4):
        norm = stat_x[b, :, half_lanes(c)]
        for k in range(2):
            v = whole[b // 2, y, b % 2, k, z].astype(F32)
            v = (v - norm[0:1]) * norm[1:2] * gain_col[k * 144:(k + 1) * 144, :]
            whole[b // 2, y, b % 2, k, z] = v.astype(BF16)
    for e in range(4):
        @pl.when(near(z, e) != x)
        def _():
            block(e, 0).wait_send()

        block(e, 1).wait_send()


    def unit(zz, yy, start, count):
        if count == 2:
            return whole.at[start // 2, yy, :, :, zz]
        return whole.at[start // 2, yy, start % 2, :, zz]

    def project(half, yy, fresh_start):
        right = jnp.concatenate([whole[half, yy, b].reshape(1152, 128) for b in range(2)], axis=1)
        left = w_t[:, pl.ds(pl.multiple_of(yy * 1152, 128), 1152)]
        part = jnp.dot(left, right, preferred_element_type=F32)
        if fresh_start:
            acc[half] = part
        else:
            acc[half] += part

    yj = [y, near(y, -1), near(y, 1), near(y, 2)]
    lent.append(lend(1))
    gathered = gather_plane(wires.branch(gather_sem), unit, peer_y, peer_z, y, z, lambda j: project(0, yj[j], j == 0), lambda j: project(1, yj[j], j == 0), True)
    next(gathered)
    next(gathered)
    next(gathered)
    own_kv.wait()
    own_wo.wait()
    shared = [
        wires(w_t.at[w_mine, :], w_t.at[w_mine, :], sibling),
        wires(w_keyval, w_t.at[kv_rows16, :], sibling),
        wires(w_out, wo.at[c, :, wo_lanes], sibling),
    ]
    next(gathered)
    next(cached)
    next(cached)
    for copy in shared[:2]:
        copy.wait_recv()
    next(gathered)
    for _ in cached:
        pass
    share = slots.reshape(16, 2, 64, 512).at[:, c]
    share_slots = wires(share, share, sibling)
    for _ in gathered:
        pass
    third, fourth = [], []
    lanes = lambda b: slice((b % 2) * 128, (b % 2) * 128 + 128)
    for b in range(4):
        kv_send[b] = acc[b // 2, 512:544, lanes(b)]
    for d in (1, 3, 2):
        third.append(wires(kv_send.at[near(x, d)], kv_recv.at[x], peer_x(d)))
    for h in range(2):
        for b in range(4):
            q_send[b, h] = acc[b // 2, h * 256:(h + 1) * 256, lanes(b)].astype(BF16)
        fourth.append([wires(q_send.at[near(x, d), h], q_recv.at[x, h], peer_x(d)) for d in (1, 3, 2)])
    for copy in third:
        copy.wait_recv()
    total = kv_send[x]
    for d in (1, 2, 3):
        total = total + kv_recv[near(x, d)]
    for k in range(2):
        kv_t[c, z, y, k] = total[k * 16:(k + 1) * 16].astype(BF16)
    kv_y = [wires(kv_t.at[c, z, y, 0], kv_t.at[c, z, y, 0], peer_y(d)) for d in (1, 3, 2)]
    kv_z = [wires(kv_t.at[c, z, y, 1], kv_t.at[c, z, y, 1], peer_z(d)) for d in (1, 3, 2)]
    line_y, line_z = kv_t.at[c, z, :, 0], kv_t.at[c, :, y, 1]
    for copy in kv_y:
        copy.wait_recv()
    kv_last = [wires(line_y, line_y, peer_z(d, dc)) for dc in (0, 1) for d in (1, 3, 2)]
    for copy in kv_z:
        copy.wait_recv()
    kv_last += [wires(line_z, line_z, peer_y(d, dc)) for dc in (0, 1) for d in (1, 3, 2)]
    kv_last += [wires(line_y, line_y, sibling), wires(line_z, line_z, sibling)]
    share_slots.wait_recv()

    @pl.loop(0, 8)
    def _(s):
        at = pl.ds(pl.multiple_of(s * 256, 256), 256)
        values_t[:, at] = slots[at, 256:512].T


    inv = 1.0 / math.sqrt(HEAD)
    cos_q, sin_q = cosine[:, half_lanes(c)], sine[:, half_lanes(c)]
    passed = []

    def pass_weights(chunks):
        for k in chunks:
            lent[k].wait_recv()
            passed.append(wires(wo.at[c, wo_rows(k), wo_other], wo.at[c, wo_rows(k), wo_other], sibling))

    def fold(s, f):
        return f(s.reshape(s.shape[0] // 8, 8, 128), axis=0)

    def rotated(u, w, cos, sin):
        return jnp.concatenate([u * cos - w * sin, w * cos + u * sin], axis=0).astype(BF16)

    stays = z // 2 == pair

    def swap(h):
        return pltpu.make_async_remote_copy(
            src_ref=heads.at[h], dst_ref=heads_all.at[y, 3 - z, h], send_sem=swap_send.at[h], recv_sem=swap_recv.at[h],
            device_id=twin, device_id_type=MESH,
        )

    def keep(h):
        return pltpu.make_async_copy(heads.at[h], heads_all.at[y, z, h], swap_recv.at[h])

    for h in range(2):
        for copy in fourth[h]:
            copy.wait_recv()
        if h:
            lent.append(lend(2))
        query = q_send[x, h].astype(F32)
        for d in (1, 2, 3):
            query = query + q_recv[near(x, d), h].astype(F32)
        queries[...] = rotated(query[0:128], query[128:256], cos_q, sin_q)

        def cached_scores(k, top):
            at = pl.ds(pl.multiple_of(k * 256, 256), 256)
            s = jnp.dot(slots[at, 0:256], queries[...], preferred_element_type=F32) * inv
            slot = k * 256 + lax.broadcasted_iota(jnp.int32, (256, 128), 0)
            s = jnp.where(slot < lengths[0], s, -1e30)
            scores[at, :] = s
            return jnp.maximum(top, fold(s, jnp.max))

        top = lax.fori_loop(0, 8, cached_scores, jnp.full((8, 128), -1e30, F32))
        if h == 0:
            for copy in kv_last:
                copy.wait_recv()
            kv = jnp.concatenate([kv_t[k].reshape(512, 128) for k in range(2)], axis=1)
            fresh = rotated(kv[0:128].astype(F32), kv[128:256].astype(F32), cosine[...], sine[...])
        s = lax.dot_general(fresh, queries[...], LEFT, preferred_element_type=F32) * inv
        t = c * 128 + lax.broadcasted_iota(jnp.int32, (256, 128), 1)
        t2 = lax.broadcasted_iota(jnp.int32, (256, 128), 0)
        s = jnp.where(t2 <= t, s, -1e30)
        scores[2048:2304, :] = s
        top = jnp.max(jnp.maximum(top, fold(s, jnp.max)), axis=0, keepdims=True)

        def exponentials(k, total):
            at = pl.ds(pl.multiple_of(k * 256, 256), 256)
            p = jnp.exp(scores[at, :] - top)
            weights[at, :] = p.astype(BF16)
            return total + fold(p, jnp.sum)

        total = jnp.sum(lax.fori_loop(0, 9, exponentials, jnp.zeros((8, 128), F32)), axis=0, keepdims=True)
        summed = jnp.dot(values_t[...], weights[0:2048, :], preferred_element_type=F32)
        summed += jnp.dot(kv[256:512], weights[2048:2304, :], preferred_element_type=F32)
        heads[h] = (summed / total).astype(BF16)
        pl.when(stays)(keep(h).start)
        pl.when(jnp.logical_not(stays))(swap(h).start)

    begun = []

    def project_out(h, j):
        if not begun:
            for copy in passed:
                copy.wait_recv()
        rights, lanes = [], []
        for k in range(2):
            block = 2 * pair + k
            rights.append(jnp.concatenate([heads_all[yj[j], block, h], heads_all[yj[j], 3 - block, h]], axis=1))
            lanes.append(pl.ds(pl.multiple_of(k * 2048 + yj[j] * 512 + h * 256, 128), 256))
        right = jnp.concatenate(rights, axis=0)
        for k in range(2):
            left = jnp.concatenate([wo[k, :, lanes[0]], wo[k, :, lanes[1]]], axis=1)
            part = jnp.dot(left, right, preferred_element_type=F32)
            if begun:
                acc_o[k] += part
            else:
                acc_o[k] = part
        begun.append(j)

    head_unit = lambda zz, yy, start, count: heads_all.at[yy, zz, start // 2, (start % 2) * 128:(start % 2 + count) * 128, :]
    pass_weights((0, 1))
    for h in range(2):
        keep(h).wait()
    heads_gather = gather_plane(
        wires.branch(gather_sem), head_unit, peer_y, peer_z, y, z, lambda j: project_out(0, j), lambda j: project_out(1, j), direct=True
    )
    next(heads_gather)
    for h in range(2):
        pl.when(jnp.logical_not(stays))(swap(h).wait_send)
    for step in range(3):
        next(heads_gather)
    shared[2].wait_recv()
    pass_weights((2,))
    for _ in heads_gather:
        pass
    for k in range(2):
        o_send[0, k] = acc_o[k, :, 128:256].astype(BF16)
    last = [
        wires(o_send.at[0, lax.rem(c + dc, 2)], o_recv.at[0, c], device(3 - x, z, y, lax.rem(c + dc, 2))) for dc in (0, 1)
    ]
    o_send[1, 1 - c] = acc_o[1 - c, :, 0:128].astype(BF16)
    last.append(wires(o_send.at[1, 1 - c], o_recv.at[1, c], sibling))
    for copy in last:
        copy.wait_recv()
    out[0, :, half_lanes(c)] = (acc_o[c, :, 0:128] + o_recv[0, c].astype(F32)).astype(BF16)
    other = o_recv[1, 1 - c].astype(F32) + o_recv[0, 1 - c].astype(F32)
    out[0, :, half_lanes(1 - c)] = other.astype(BF16)

    wires.finish()
    assert wires.used <= RECV and len(locals_) <= 8


def body(tokens, gain, w_query, w_keyval, w_out, cache, lengths):
    hbm = pl.BlockSpec(memory_space=pl.ANY)
    vmem = pl.BlockSpec(memory_space=pltpu.VMEM)
    smem = pl.BlockSpec(memory_space=pltpu.SMEM)
    out = pl.pallas_call(
        kernel,
        out_shape=jax.ShapeDtypeStruct((1, 576, 256), BF16),
        in_specs=[hbm, vmem, hbm, hbm, hbm, hbm, smem],
        out_specs=vmem,
        scratch_shapes=[
            pltpu.VMEM((576, 256), BF16),
            pltpu.VMEM((4, 144, 256), BF16),
            pltpu.VMEM((4, 8, 256), F32),
            pltpu.VMEM((8, 8, 256), F32),
            pltpu.VMEM((4, 8, 256), F32),
            pltpu.VMEM((288, 128), F32),
            pltpu.VMEM((2, 4, 2, 2, 4, 144, 128), BF16),
            pltpu.VMEM((4608, 256), BF16),
            pltpu.VMEM((544, 4608), BF16),
            pltpu.VMEM((2, 576, 4096), BF16),
            pltpu.VMEM((2, 544, 256), F32),
            pltpu.VMEM((4, 2, 256, 128), BF16),
            pltpu.VMEM((4, 2, 256, 128), BF16),
            pltpu.VMEM((4, 32, 128), F32),
            pltpu.VMEM((4, 32, 128), F32),
            pltpu.VMEM((2, 4, 4, 2, 16, 128), BF16),
            pltpu.VMEM((2048, 512), BF16),
            pltpu.VMEM((256, 2048), BF16),
            pltpu.VMEM((128, 256), F32),
            pltpu.VMEM((128, 256), F32),
            pltpu.VMEM((2304, 128), F32),
            pltpu.VMEM((2304, 128), BF16),
            pltpu.VMEM((256, 128), BF16),
            pltpu.VMEM((2, 256, 128), BF16),
            pltpu.VMEM((4, 4, 2, 256, 128), BF16),
            pltpu.VMEM((2, 576, 256), F32),
            pltpu.VMEM((2, 2, 576, 128), BF16),
            pltpu.VMEM((2, 2, 576, 128), BF16),
            pltpu.SemaphoreType.DMA((POOL,)),
            pltpu.SemaphoreType.DMA((RECV,)),
            pltpu.SemaphoreType.DMA((40,)),
            pltpu.SemaphoreType.DMA((8,)),
            pltpu.SemaphoreType.DMA((8,)),
            pltpu.SemaphoreType.DMA((8,)),
            pltpu.SemaphoreType.DMA((2,)),
            pltpu.SemaphoreType.DMA((2,)),
        ],
        compiler_params=pltpu.CompilerParams(
            collective_id=0, has_side_effects=True, vmem_limit_bytes=56 * 1024 * 1024
        ),
    )(
        jnp.swapaxes(tokens, 1, 2), gain.reshape(144, 128), w_query, w_keyval.T, w_out.T, cache, lengths
    )
    return jnp.swapaxes(out, 1, 2)


def solution(mesh):
    return jax.shard_map(
        body,
        mesh=mesh,
        in_specs=(
            P("gx", None, "yz"),
            P(),
            P("gx", "yz"),
            P("gx", "yz"),
            P("gx", "yz"),
            P("gx", "yz", None),
            P("gx"),
        ),
        out_specs=P("gx", None, "yz"),
        check_vma=False,
    )
```

```python
import math

import jax
import jax.numpy as jnp
from jax import lax
from jax.experimental import pallas as pl
from jax.experimental.pallas import tpu as pltpu
from jax.sharding import PartitionSpec as P

MESH = pl.DeviceIdType.MESH
HEAD = 256
F32 = jnp.float32
BF16 = jnp.bfloat16
LEFT = (((0,), (0,)), ((), ()))
POOL = 72
RECV = 77


class Wires:
    def __init__(self, send, recv, pool):
        self.send, self.recv, self.pool, self.used, self.all = send, recv, pool, 0, []

    def __call__(self, src, dst, target):
        self.used += 1
        return self.start(src, dst, target, self.recv.at[self.used - 1])

    def branch(self, recv):
        slots = iter(range(64))
        return lambda src, dst, target: self.start(src, dst, target, recv.at[next(slots)])

    def start(self, src, dst, target, recv):
        n = len(self.all)
        if n >= self.pool:
            self.all[n - self.pool].wait_send()
        copy = pltpu.make_async_remote_copy(
            src_ref=src, dst_ref=dst, send_sem=self.send.at[n % self.pool], recv_sem=recv,
            device_id=target, device_id_type=MESH,
        )
        copy.start()
        self.all.append(copy)
        return copy

    def finish(self):
        for copy in self.all[-self.pool:]:
            copy.wait_send()


def near(v, d):
    return lax.rem(v + d + 4, 4)


def gather_plane(wires, unit, peer_y, peer_z, y, z, on_a=lambda j: None, on_b=lambda j: None, direct=False):
    yj = [y, near(y, -1), near(y, 1), near(y, 2)]
    zj = [z, near(z, -1), near(z, 1), near(z, 2)]

    def send(ref, target):
        return wires(ref, ref, target)

    zp, zm, yp, ym = [None] * 4, [None] * 4, [None] * 4, [None] * 4
    zfp, zfm, yfp, yfm = [None] * 4, [None] * 4, [None] * 4, [None] * 4

    def spread_a(j):
        zp[j] = send(unit(z, yj[j], 0, 2), peer_z(1))
        zm[j] = send(unit(z, yj[j], 0, 2), peer_z(-1))

    def spread_b(j):
        yp[j] = send(unit(zj[j], y, 2, 2), peer_y(1))
        ym[j] = send(unit(zj[j], y, 2, 2), peer_y(-1))

    def pass_a(j):
        zp[j].wait_recv()
        zfp[j] = send(unit(zj[1], yj[j], 0, 1), peer_z(1))
        zm[j].wait_recv()
        zfm[j] = send(unit(zj[2], yj[j], 1, 1), peer_z(-1))

    def pass_b(j):
        yp[j].wait_recv()
        yfp[j] = send(unit(zj[j], yj[1], 2, 1), peer_y(1))
        ym[j].wait_recv()
        yfm[j] = send(unit(zj[j], yj[2], 3, 1), peer_y(-1))

    a1p = send(unit(z, y, 0, 2), peer_y(1))
    b1p = send(unit(z, y, 2, 2), peer_z(1))
    a1m = send(unit(z, y, 0, 2), peer_y(-1))
    b1m = send(unit(z, y, 2, 2), peer_z(-1))
    spread_a(0)
    spread_b(0)
    if direct:
        a2p = send(unit(z, y, 0, 2), peer_y(2))
        b2p = send(unit(z, y, 2, 2), peer_z(2))
    yield
    a1p.wait_recv()
    if not direct:
        a2p = send(unit(z, yj[1], 0, 1), peer_y(1))
    spread_a(1)
    b1p.wait_recv()
    if not direct:
        b2p = send(unit(zj[1], y, 2, 1), peer_z(1))
    spread_b(1)
    yield
    a1m.wait_recv()
    a2 = [a2p]
    if not direct:
        a2.append(send(unit(z, yj[2], 1, 1), peer_y(-1)))
    spread_a(2)
    b1m.wait_recv()
    b2 = [b2p]
    if not direct:
        b2.append(send(unit(zj[2], y, 3, 1), peer_z(-1)))
    spread_b(2)
    yield
    pass_a(0)
    pass_b(0)
    yield
    for copy in a2:
        copy.wait_recv()
    spread_a(3)
    for copy in b2:
        copy.wait_recv()
    spread_b(3)
    yield
    for j in range(1, 4):
        pass_a(j)
        pass_b(j)
        if j == 2:
            on_b(0)
            zfp[0].wait_recv()
            zfm[0].wait_recv()
            on_a(0)
        yield
    for j in (1, 2):
        zfp[j].wait_recv()
        zfm[j].wait_recv()
        on_a(j)
    on_b(1)
    on_b(2)
    for copy in (zfp[3], zfm[3]):
        copy.wait_recv()
    on_a(3)
    for j in range(4):
        yfp[j].wait_recv()
        yfm[j].wait_recv()
    on_b(3)


def gather_direct(wires, unit, peer_y, peer_z, y, z, on_a=lambda j: None, on_b=lambda j: None):
    yj = [y, near(y, -1), near(y, 1), near(y, 2)]
    zj = [z, near(z, -1), near(z, 1), near(z, 2)]
    ways = (1, -1, 2)

    def send(ref, peer):
        return [wires(ref, ref, peer(d)) for d in ways]

    own_a, own_b = unit(z, y, 0, 2), unit(z, y, 2, 2)
    a1, b1 = send(own_a, peer_y), send(own_b, peer_z)
    a2, b2 = [send(own_a, peer_z)], [send(own_b, peer_y)]
    yield
    for j in range(3):
        a1[j].wait_recv()
        a2.append(send(unit(z, yj[j + 1], 0, 2), peer_z))
        b1[j].wait_recv()
        b2.append(send(unit(zj[j + 1], y, 2, 2), peer_y))
        yield
    on_b(0)
    for j in range(4):
        for copy in a2[j]:
            copy.wait_recv()
        on_a(j)
        yield
    for j in (1, 2, 3):
        for k in range(4):
            b2[k][j - 1].wait_recv()
        on_b(j)


def gather_lines(wires, unit, peer_y, peer_z, y, z):
    yj = [y, near(y, -1), near(y, 1), near(y, 2)]
    zj = [z, near(z, -1), near(z, 1), near(z, 2)]

    def send(ref, target):
        return wires(ref, ref, target)

    def spread(j):
        ref = unit(zj[j], y, None)
        return [send(ref, peer_y(1)), send(ref, peer_y(-1))]

    def hand_on(j, pair):
        pair[0].wait_recv()
        first = send(unit(zj[j], yj[1], 0), peer_y(1))
        pair[1].wait_recv()
        return [first, send(unit(zj[j], yj[2], 1), peer_y(-1))]

    own = unit(z, y, None)
    along = [send(own, peer_z(d)) for d in (1, -1, 2)]
    near_y = [spread(0)]
    yield
    for j in (1, 2):
        along[j - 1].wait_recv()
        near_y.append(spread(j))
    far_y = [hand_on(0, near_y[0])]
    yield
    along[2].wait_recv()
    near_y.append(spread(3))
    for j in (1, 2, 3):
        yield
        far_y.append(hand_on(j, near_y[j]))
    yield
    for pair in far_y:
        for copy in pair:
            copy.wait_recv()


def kernel(
    tokens, gain, w_query, w_keyval, w_out, cache, lengths, out,
    mine, raw, stat_y, stat_z, stat_x, gain_col, whole, w_rows, w_t, wo, acc, q_send, q_recv, kv_send, kv_recv,
    kv_t, slots, values_t, cosine, sine, scores, weights, queries, heads, heads_all, acc_o, o_send, o_recv,
    send_sem, recv_sem, gather_sem, local_sem, block_send, block_recv, swap_send, swap_recv,
):
    x = lax.axis_index("gx")
    yz = lax.axis_index("yz")
    z, y, c = yz // 8, (yz // 2) % 4, yz % 2

    def device(xx, zz, yy, cc):
        return (xx, zz * 8 + yy * 2 + cc)

    peer_x = lambda d, dc=0: device(near(x, d), z, y, lax.rem(c + dc, 2))
    peer_y = lambda d, dc=0: device(x, z, near(y, d), lax.rem(c + dc, 2))
    peer_z = lambda d, dc=0: device(x, near(z, d), y, lax.rem(c + dc, 2))
    sibling = device(x, z, y, 1 - c)

    barrier = pltpu.get_barrier_semaphore()
    peers = [sibling]
    for d in (1, 2, 3):
        peers += [peer_x(d), peer_x(d, 1), peer_z(d), peer_z(d, 1), peer_y(d), peer_y(d, 1)]
    twin = device(3 - x, 3 - z, y, c)
    peers.append(twin)
    for p in peers:
        pl.semaphore_signal(barrier, inc=1, device_id=p, device_id_type=MESH)

    locals_ = []

    def local(src, dst):
        copy = pltpu.make_async_copy(src, dst, local_sem.at[len(locals_)])
        copy.start()
        locals_.append(copy)
        return copy

    quarter = lambda k: pl.ds(pl.multiple_of(k * 144, 16), 144)
    own_mine = local(tokens.at[0], mine)
    slot_rows = pl.ds(pl.multiple_of(yz * 64, 64), 64)
    own_slots = local(cache.at[0], slots.at[slot_rows, :])
    own_raw = local(tokens.at[0, quarter(z), :], raw.at[z])
    own_rows = local(w_query, w_rows)
    kv_rows16 = pl.ds(pl.multiple_of(512 + c * 16, 16), 16)
    own_kv = local(w_keyval, w_t.at[kv_rows16, :])
    pair = x // 2
    partner = device(x + 1 - 2 * (x % 2), z, y, c)
    wo_lanes = pl.ds(pl.multiple_of((x % 2) * 2048, 128), 2048)
    wo_other = pl.ds(pl.multiple_of((1 - x % 2) * 2048, 128), 2048)
    own_wo = local(w_out, wo.at[c, :, wo_lanes])
    wo_rows = lambda k: pl.ds((0, 96, 432)[k], (96, 336, 144)[k])

    def lend(k):
        return wires(w_out.at[wo_rows(k), :], wo.at[c, wo_rows(k), wo_lanes], partner)


    pl.semaphore_wait(barrier, len(peers))
    wires = Wires(send_sem, recv_sem, POOL)
    first = [wires(tokens.at[0, quarter(near(z, d)), :], raw.at[z], peer_z(d)) for d in (1, 3, 2)]

    spot = whole.at[x // 2, y, x % 2, c, z]
    half_lanes = lambda k: pl.ds(pl.multiple_of(k * 128, 128), 128)

    def block(e, dc):
        i, cc = near(z, e), lax.rem(c + dc, 2)
        return pltpu.make_async_remote_copy(
            src_ref=raw.at[i, :, half_lanes(cc)], dst_ref=spot, send_sem=block_send.at[e * 2 + dc],
            recv_sem=block_recv.at[x * 2 + c], device_id=device(i, z, y, cc), device_id_type=MESH,
        )

    def start_block(e):
        @pl.when(near(z, e) == x)
        def _():
            pltpu.make_async_copy(raw.at[x, :, half_lanes(c)], spot, block_recv.at[x * 2 + c]).start()

        @pl.when(near(z, e) != x)
        def _():
            block(e, 0).start()

        block(e, 1).start()

    own_raw.wait()
    start_block(0)
    lent = [lend(0)]

    own_mine.wait()
    v = mine[...].astype(F32)
    mean = jnp.sum(v, axis=0, keepdims=True) * (1.0 / 576)
    square = jnp.sum((v - mean) * (v - mean), axis=0, keepdims=True)
    row = lax.broadcasted_iota(jnp.int32, (8, 256), 0)

    def join(ref, count, size):
        means = [ref[k][0:1] for k in range(count)]
        mid = sum(means[1:], means[0]) * (1.0 / count)
        total = sum([ref[k][1:2] for k in range(1, count)], ref[0][1:2])
        for m in means:
            total = total + size * (m - mid) * (m - mid)
        return mid, total

    stat_y[y] = jnp.where(row == 0, mean, square)
    stat_1 = [wires(stat_y.at[y], stat_y.at[y], peer_y(d)) for d in (1, 3, 2)]
    own_slots.wait()

    def cache_unit(zz, yy, part):
        at = (zz * 8 + yy * 2 + c) * 64 + (0 if part is None else part * 32)
        return slots.at[pl.ds(pl.multiple_of(at, 32), 64 if part is None else 32), :]

    cached = gather_lines(wires, cache_unit, peer_y, peer_z, y, z)
    next(cached)

    lane = lax.broadcasted_iota(jnp.int32, (16, 128), 1)
    sub = lax.broadcasted_iota(jnp.int32, (16, 128), 0)

    for k in range(18):
        g = x * 288 + y * 72 + (k // 9) * 36 + z * 9 + k % 9
        line = jnp.broadcast_to(gain[pl.ds(g // 8, 1), :], (16, 128))
        col = jnp.sum(jnp.where(lane == sub + (g % 8) * 16, line, 0.0), axis=1, keepdims=True)
        gain_col[k * 16:(k + 1) * 16, :] = jnp.broadcast_to(col, (16, 128))

    freq = jnp.exp(
        lax.broadcasted_iota(jnp.int32, (128, 256), 0).astype(F32) * (-2.0 * math.log(10000.0) / HEAD)
    )
    angle = (lengths[0] + lax.broadcasted_iota(jnp.int32, (128, 256), 1)).astype(F32) * freq
    cosine[...] = jnp.cos(angle)
    sine[...] = jnp.sin(angle)
    for copy in stat_1:
        copy.wait_recv()
    mean, square = join(stat_y, 4, 576.0)
    me = z * 2 + c
    stat_z[me] = jnp.where(row == 0, mean, square)
    stat_2 = []
    for d in (1, 3, 2):
        for dc in (0, 1):
            stat_2.append(wires(stat_z.at[me], stat_z.at[me], peer_z(d, dc)))
    stat_2.append(wires(stat_z.at[me], stat_z.at[me], sibling))
    first[0].wait_recv()
    start_block(3)
    first[1].wait_recv()
    start_block(1)
    next(cached)
    for copy in stat_2:
        copy.wait_recv()
    mean, square = join(stat_z, 8, 2304.0)
    stat_x[x] = jnp.where(row == 0, mean, lax.rsqrt(square * (1.0 / 18432) + 1e-6))
    stat_3 = [wires(stat_x.at[x], stat_x.at[x], peer_x(d)) for d in (1, 3, 2)]
    first[2].wait_recv()
    start_block(2)
    next(cached)
    next(cached)
    own_rows.wait()
    w_mine = pl.ds(pl.multiple_of(c * 256, 256), 256)

    @pl.loop(0, 18)
    def _(s):
        at = pl.ds(pl.multiple_of(s * 256, 256), 256)
        w_t[w_mine, at] = w_rows[at, :].T

    for k in range(8):
        pltpu.make_async_copy(raw.at[0, :, 0:128], whole.at[k // 4, y, (k // 2) % 2, k % 2, z], block_recv.at[k]).wait()
    for copy in stat_3:
        copy.wait_recv()
    for b in range(4):
        norm = stat_x[b, :, half_lanes(c)]
        for k in range(2):
            v = whole[b // 2, y, b % 2, k, z].astype(F32)
            v = (v - norm[0:1]) * norm[1:2] * gain_col[k * 144:(k + 1) * 144, :]
            whole[b // 2, y, b % 2, k, z] = v.astype(BF16)
    for e in range(4):
        @pl.when(near(z, e) != x)
        def _():
            block(e, 0).wait_send()

        block(e, 1).wait_send()


    def unit(zz, yy, start, count):
        if count == 2:
            return whole.at[start // 2, yy, :, :, zz]
        return whole.at[start // 2, yy, start % 2, :, zz]

    def project(half, yy, fresh_start):
        right = jnp.concatenate([whole[half, yy, b].reshape(1152, 128) for b in range(2)], axis=1)
        left = w_t[:, pl.ds(pl.multiple_of(yy * 1152, 128), 1152)]
        part = jnp.dot(left, right, preferred_element_type=F32)
        if fresh_start:
            acc[half] = part
        else:
            acc[half] += part

    yj = [y, near(y, -1), near(y, 1), near(y, 2)]
    lent.append(lend(1))
    gathered = gather_plane(wires.branch(gather_sem), unit, peer_y, peer_z, y, z, lambda j: project(0, yj[j], j == 0), lambda j: project(1, yj[j], j == 0), True)
    next(gathered)
    next(gathered)
    next(gathered)
    own_kv.wait()
    own_wo.wait()
    shared = [
        wires(w_t.at[w_mine, :], w_t.at[w_mine, :], sibling),
        wires(w_keyval, w_t.at[kv_rows16, :], sibling),
        wires(w_out, wo.at[c, :, wo_lanes], sibling),
    ]
    next(gathered)
    next(cached)
    next(cached)
    for copy in shared[:2]:
        copy.wait_recv()
    next(gathered)
    for _ in cached:
        pass
    share = slots.reshape(16, 2, 64, 512).at[:, c]
    share_slots = wires(share, share, sibling)
    for _ in gathered:
        pass
    third, fourth = [], []
    lanes = lambda b: slice((b % 2) * 128, (b % 2) * 128 + 128)
    for b in range(4):
        kv_send[b] = acc[b // 2, 512:544, lanes(b)]
    for d in (1, 3, 2):
        third.append(wires(kv_send.at[near(x, d)], kv_recv.at[x], peer_x(d)))
    for h in range(2):
        for b in range(4):
            q_send[b, h] = acc[b // 2, h * 256:(h + 1) * 256, lanes(b)].astype(BF16)
        fourth.append([wires(q_send.at[near(x, d), h], q_recv.at[x, h], peer_x(d)) for d in (1, 3, 2)])
    for copy in third:
        copy.wait_recv()
    total = kv_send[x]
    for d in (1, 2, 3):
        total = total + kv_recv[near(x, d)]
    for k in range(2):
        kv_t[c, z, y, k] = total[k * 16:(k + 1) * 16].astype(BF16)
    kv_y = [wires(kv_t.at[c, z, y, 0], kv_t.at[c, z, y, 0], peer_y(d)) for d in (1, 3, 2)]
    kv_z = [wires(kv_t.at[c, z, y, 1], kv_t.at[c, z, y, 1], peer_z(d)) for d in (1, 3, 2)]
    line_y, line_z = kv_t.at[c, z, :, 0], kv_t.at[c, :, y, 1]
    for copy in kv_y:
        copy.wait_recv()
    kv_last = [wires(line_y, line_y, peer_z(d, dc)) for dc in (0, 1) for d in (1, 3, 2)]
    for copy in kv_z:
        copy.wait_recv()
    kv_last += [wires(line_z, line_z, peer_y(d, dc)) for dc in (0, 1) for d in (1, 3, 2)]
    kv_last += [wires(line_y, line_y, sibling), wires(line_z, line_z, sibling)]
    share_slots.wait_recv()

    @pl.loop(0, 8)
    def _(s):
        at = pl.ds(pl.multiple_of(s * 256, 256), 256)
        values_t[:, at] = slots[at, 256:512].T


    inv = 1.0 / math.sqrt(HEAD)
    cos_q, sin_q = cosine[:, half_lanes(c)], sine[:, half_lanes(c)]
    passed = []

    def pass_weights(chunks):
        for k in chunks:
            lent[k].wait_recv()
            passed.append(wires(wo.at[c, wo_rows(k), wo_other], wo.at[c, wo_rows(k), wo_other], sibling))

    def fold(s, f):
        return f(s.reshape(s.shape[0] // 8, 8, 128), axis=0)

    def rotated(u, w, cos, sin):
        return jnp.concatenate([u * cos - w * sin, w * cos + u * sin], axis=0).astype(BF16)

    stays = z // 2 == pair

    def swap(h):
        return pltpu.make_async_remote_copy(
            src_ref=heads.at[h], dst_ref=heads_all.at[y, 3 - z, h], send_sem=swap_send.at[h], recv_sem=swap_recv.at[h],
            device_id=twin, device_id_type=MESH,
        )

    def keep(h):
        return pltpu.make_async_copy(heads.at[h], heads_all.at[y, z, h], swap_recv.at[h])

    for h in range(2):
        for copy in fourth[h]:
            copy.wait_recv()
        if not h:
            lent.append(lend(2))
        query = q_send[x, h].astype(F32)
        for d in (1, 2, 3):
            query = query + q_recv[near(x, d), h].astype(F32)
        queries[...] = rotated(query[0:128], query[128:256], cos_q, sin_q)

        def cached_scores(k, top):
            at = pl.ds(pl.multiple_of(k * 256, 256), 256)
            s = jnp.dot(slots[at, 0:256], queries[...], preferred_element_type=F32) * inv
            slot = k * 256 + lax.broadcasted_iota(jnp.int32, (256, 128), 0)
            s = jnp.where(slot < lengths[0], s, -1e30)
            scores[at, :] = s
            return jnp.maximum(top, fold(s, jnp.max))

        top = lax.fori_loop(0, 8, cached_scores, jnp.full((8, 128), -1e30, F32))
        if h == 0:
            for copy in kv_last:
                copy.wait_recv()
            kv = jnp.concatenate([kv_t[k].reshape(512, 128) for k in range(2)], axis=1)
            fresh = rotated(kv[0:128].astype(F32), kv[128:256].astype(F32), cosine[...], sine[...])
        s = lax.dot_general(fresh, queries[...], LEFT, preferred_element_type=F32) * inv
        t = c * 128 + lax.broadcasted_iota(jnp.int32, (256, 128), 1)
        t2 = lax.broadcasted_iota(jnp.int32, (256, 128), 0)
        s = jnp.where(t2 <= t, s, -1e30)
        scores[2048:2304, :] = s
        top = jnp.max(jnp.maximum(top, fold(s, jnp.max)), axis=0, keepdims=True)

        def exponentials(k, total):
            at = pl.ds(pl.multiple_of(k * 256, 256), 256)
            p = jnp.exp(scores[at, :] - top)
            weights[at, :] = p.astype(BF16)
            return total + fold(p, jnp.sum)

        total = jnp.sum(lax.fori_loop(0, 9, exponentials, jnp.zeros((8, 128), F32)), axis=0, keepdims=True)
        summed = jnp.dot(values_t[...], weights[0:2048, :], preferred_element_type=F32)
        summed += jnp.dot(kv[256:512], weights[2048:2304, :], preferred_element_type=F32)
        heads[h] = (summed / total).astype(BF16)
        pl.when(stays)(keep(h).start)
        pl.when(jnp.logical_not(stays))(swap(h).start)

    begun = []

    def project_out(h, j):
        if not begun:
            for copy in passed:
                copy.wait_recv()
        rights, lanes = [], []
        for k in range(2):
            block = 2 * pair + k
            rights.append(jnp.concatenate([heads_all[yj[j], block, h], heads_all[yj[j], 3 - block, h]], axis=1))
            lanes.append(pl.ds(pl.multiple_of(k * 2048 + yj[j] * 512 + h * 256, 128), 256))
        right = jnp.concatenate(rights, axis=0)
        for k in range(2):
            left = jnp.concatenate([wo[k, :, lanes[0]], wo[k, :, lanes[1]]], axis=1)
            part = jnp.dot(left, right, preferred_element_type=F32)
            if begun:
                acc_o[k] += part
            else:
                acc_o[k] = part
        begun.append(j)

    head_unit = lambda zz, yy, start, count: heads_all.at[yy, zz, start // 2, (start % 2) * 128:(start % 2 + count) * 128, :]
    pass_weights((0, 1))
    for h in range(2):
        keep(h).wait()
    heads_gather = gather_plane(
        wires.branch(gather_sem), head_unit, peer_y, peer_z, y, z, lambda j: project_out(0, j), lambda j: project_out(1, j), direct=True
    )
    next(heads_gather)
    for h in range(2):
        pl.when(jnp.logical_not(stays))(swap(h).wait_send)
    for step in range(2):
        next(heads_gather)
    shared[2].wait_recv()
    pass_weights((2,))
    for _ in heads_gather:
        pass
    last = []
    for dc in (0, 1):
        cc = lax.rem(c + dc, 2)
        o_send[0, cc] = acc_o[cc, :, 128:256].astype(BF16)
        last.append(wires(o_send.at[0, cc], o_recv.at[0, c], device(3 - x, z, y, cc)))
    o_send[1, 1 - c] = acc_o[1 - c, :, 0:128].astype(BF16)
    last.append(wires(o_send.at[1, 1 - c], o_recv.at[1, c], sibling))
    for copy in last:
        copy.wait_recv()
    out[0, :, half_lanes(c)] = (acc_o[c, :, 0:128] + o_recv[0, c].astype(F32)).astype(BF16)
    other = o_recv[1, 1 - c].astype(F32) + o_recv[0, 1 - c].astype(F32)
    out[0, :, half_lanes(1 - c)] = other.astype(BF16)

    wires.finish()
    assert wires.used <= RECV and len(locals_) <= 8


def body(tokens, gain, w_query, w_keyval, w_out, cache, lengths):
    hbm = pl.BlockSpec(memory_space=pl.ANY)
    vmem = pl.BlockSpec(memory_space=pltpu.VMEM)
    smem = pl.BlockSpec(memory_space=pltpu.SMEM)
    out = pl.pallas_call(
        kernel,
        out_shape=jax.ShapeDtypeStruct((1, 576, 256), BF16),
        in_specs=[hbm, vmem, hbm, hbm, hbm, hbm, smem],
        out_specs=vmem,
        scratch_shapes=[
            pltpu.VMEM((576, 256), BF16),
            pltpu.VMEM((4, 144, 256), BF16),
            pltpu.VMEM((4, 8, 256), F32),
            pltpu.VMEM((8, 8, 256), F32),
            pltpu.VMEM((4, 8, 256), F32),
            pltpu.VMEM((288, 128), F32),
            pltpu.VMEM((2, 4, 2, 2, 4, 144, 128), BF16),
            pltpu.VMEM((4608, 256), BF16),
            pltpu.VMEM((544, 4608), BF16),
            pltpu.VMEM((2, 576, 4096), BF16),
            pltpu.VMEM((2, 544, 256), F32),
            pltpu.VMEM((4, 2, 256, 128), BF16),
            pltpu.VMEM((4, 2, 256, 128), BF16),
            pltpu.VMEM((4, 32, 128), F32),
            pltpu.VMEM((4, 32, 128), F32),
            pltpu.VMEM((2, 4, 4, 2, 16, 128), BF16),
            pltpu.VMEM((2048, 512), BF16),
            pltpu.VMEM((256, 2048), BF16),
            pltpu.VMEM((128, 256), F32),
            pltpu.VMEM((128, 256), F32),
            pltpu.VMEM((2304, 128), F32),
            pltpu.VMEM((2304, 128), BF16),
            pltpu.VMEM((256, 128), BF16),
            pltpu.VMEM((2, 256, 128), BF16),
            pltpu.VMEM((4, 4, 2, 256, 128), BF16),
            pltpu.VMEM((2, 576, 256), F32),
            pltpu.VMEM((2, 2, 576, 128), BF16),
            pltpu.VMEM((2, 2, 576, 128), BF16),
            pltpu.SemaphoreType.DMA((POOL,)),
            pltpu.SemaphoreType.DMA((RECV,)),
            pltpu.SemaphoreType.DMA((40,)),
            pltpu.SemaphoreType.DMA((8,)),
            pltpu.SemaphoreType.DMA((8,)),
            pltpu.SemaphoreType.DMA((8,)),
            pltpu.SemaphoreType.DMA((2,)),
            pltpu.SemaphoreType.DMA((2,)),
        ],
        compiler_params=pltpu.CompilerParams(
            collective_id=0, has_side_effects=True, vmem_limit_bytes=56 * 1024 * 1024
        ),
    )(
        jnp.swapaxes(tokens, 1, 2), gain.reshape(144, 128), w_query, w_keyval.T, w_out.T, cache, lengths
    )
    return jnp.swapaxes(out, 1, 2)


def solution(mesh):
    return jax.shard_map(
        body,
        mesh=mesh,
        in_specs=(
            P("gx", None, "yz"),
            P(),
            P("gx", "yz"),
            P("gx", "yz"),
            P("gx", "yz"),
            P("gx", "yz", None),
            P("gx"),
        ),
        out_specs=P("gx", None, "yz"),
        check_vma=False,
    )
```
